32 devices in a mesh: section: 2 (over x), dp: 4 (over y, core), mp: 4 (over z).
Axes of the slice: x: 2, y: 2, z: 4, core: 2. Of those that a mesh axis runs over, the one named last changes fastest.
Arguments:
- hidden: bfloat16 [2, 4, 256, 5120], P('section', 'dp'), may hold values from -6 to 6
- gain: float32 [2, 5120], P('section'), may hold values from 0.5 to 2
- w_first: bfloat16 [2, 5120, 2560], P('section', 'dp', 'mp'), may hold values from -0.078125 to 0.078125
- w_second: bfloat16 [2, 5120, 2560], P('section', 'dp', 'mp'), may hold values from -0.078125 to 0.078125
- lengths: int32 [4, 2], P('dp'), may hold values from 32 to 256, as said below
- cotangent: bfloat16 [2, 4, 256, 5120], P('section', 'dp'), may hold values from -6 to 6
Outputs:
- result: bfloat16 [2, 4, 256, 5120], P('section', 'dp')
- d_hidden: bfloat16 [2, 4, 256, 5120], P('section', 'dp')
- d_gain: float32 [2, 5120], P('section', 'dp')
- d_first: float32 [2, 5120, 2560], P('section', 'dp', 'mp')
- d_second: float32 [2, 5120, 2560], P('section', 'dp', 'mp')
The draws below stay inside these ranges and needn't reach their ends.
Inputs may be any that keep to these rules, and one draw needn't show every extreme that they name: `lengths`: each row's source count and target count; positions at or past a count are padding.
All inputs are finite; a program needn't handle non-finite values.
Results may differ from the reference program's by a relative error of at most 0.017.
Values may be sent and summed in bfloat16 or wider, within the bound.
No kernel may reach another device: no remote copies, remote signals or barrier semaphores. Data moves between devices by JAX's collectives and lax.ppermute only.
A program may use at most 128 MiB of HBM per device.

```python
import math
import jax
import jax.numpy as jnp
from jax import lax

D = 5120
HEAD = 128
SEQS = 1
LEN = 256
HD = 2560
BATCH = 4
N_DP = 4


def draw_gain(key, part):
    return jax.random.uniform(key, (2, D), jnp.float32, 0.5, 1.5)


def draw_lengths(key, part):
    lowest = max(LEN // 8, 1)
    counts = jax.random.randint(key, (BATCH, 2), lowest, LEN + 1)
    shuffled = jax.random.permutation(jax.random.fold_in(key, 11), BATCH)
    counts = counts.at[shuffled[0]].set(LEN)
    counts = counts.at[shuffled[1]].set(lowest)
    return counts.astype(jnp.int32)


def spiked(drawn, rng, source, target, parts, factor):
    owner, partner = [(jnp.arange(drawn.shape[dim]) // (drawn.shape[dim] // parts)).reshape([-1 if axis == dim else 1 for axis in range(drawn.ndim)]) for dim in (source, target)]
    chosen = jax.random.permutation(rng, parts)[partner]
    strong = (owner == chosen) | (owner == (partner + parts // 2) % parts)
    return jnp.where(strong, factor * drawn, drawn)


def shard_levels(stream_key, dims, shards, least, largest):
    level, own = 1.0, jax.random.fold_in(stream_key, 6)
    for position, parts in shards:
        draws = jnp.exp(jax.random.uniform(jax.random.fold_in(own, position), (parts,), jnp.float32, least / len(shards), largest / len(shards)))
        level = level * jnp.repeat(draws, dims[position] // parts).reshape([-1 if axis == position else 1 for axis in range(len(dims))])
    return level


def centred(rng, dims, deviation, reach, split=(), kind=jnp.bfloat16):
    level = shard_levels(rng, dims, split, -0.22, 0.18) if split else 1.0
    drawn = jax.random.normal(rng, dims, jnp.float32) * deviation * level
    return jnp.minimum(jnp.maximum(drawn, -reach), reach).astype(kind)


def noise_with(key, shape, scale, most, cuts, heavy, kind=jnp.bfloat16):
    array = scale * jax.random.normal(key, shape, jnp.float32)
    if cuts:
        array = array * shard_levels(key, shape, cuts, -0.22, 0.18)
    return jnp.clip(spiked(array, jax.random.fold_in(key, 3), *heavy), -most, most).astype(kind)


def setup_inputs(seed: int = 0) -> dict:
    seeds = jax.random.split(jax.random.key(seed), 7)
    hidden = noise_with(seeds[0], (2, BATCH, LEN, D), 1.0, 6.0, ((0, 2), (1, 4)), (1, 3, 4, 2.0))
    gain = draw_gain(jax.random.fold_in(seeds[6], 71), 0)
    w_first = centred(seeds[2], (2, D, HD), D ** -0.5, 0.078125, ((0, 2), (1, 4), (2, 4)))
    w_second = centred(seeds[3], (2, D, HD), D ** -0.5, 0.078125, ((0, 2), (1, 4), (2, 4)))
    lengths = draw_lengths(jax.random.fold_in(seeds[6], 71), 0)
    cotangent = centred(seeds[5], (2, BATCH, LEN, D), 1.0, 6.0, ((0, 2), (1, 4)))
    return dict(hidden=hidden, gain=gain, w_first=w_first, w_second=w_second, lengths=lengths, cotangent=cotangent)


EPS = 1e-06
MASKED = -1e+30

def normalize(states):
    wide = states.astype(jnp.float32)
    inverse = lax.rsqrt(lax.optimization_barrier(jnp.mean(wide * wide, axis=-1, keepdims=True)) + EPS)
    return (wide * inverse, inverse)

def project(left, right):
    flat = left.reshape(-1, left.shape[-1])
    return jnp.dot(flat, right, preferred_element_type=jnp.float32).reshape(left.shape[:-1] + (right.shape[-1],))

def project_back(left, right):
    flat = left.reshape(-1, left.shape[-1])
    return jnp.dot(flat, right.T, preferred_element_type=jnp.float32).reshape(left.shape[:-1] + (right.shape[0],))

def grouped_outer(left, right):
    span = SEQS * LEN
    left_rows = left.reshape(-1, left.shape[-1])
    right_rows = right.reshape(-1, right.shape[-1])
    total = jnp.zeros((left_rows.shape[1], right_rows.shape[1]), jnp.float32)
    for member in range(N_DP):
        piece = jnp.dot(left_rows[member * span:(member + 1) * span].T, right_rows[member * span:(member + 1) * span], preferred_element_type=jnp.float32)
        total = total + lax.optimization_barrier(piece.astype(jnp.bfloat16)).astype(jnp.float32)
    return total

def grouped_vector(product):
    pieces = lax.optimization_barrier(jnp.sum(product.reshape(N_DP, SEQS * LEN, product.shape[-1]), axis=1))
    pieces = lax.optimization_barrier(pieces.astype(jnp.bfloat16)).astype(jnp.float32)
    return lax.optimization_barrier(jnp.sum(pieces, axis=0))

def split_heads(values_in):
    batch_size, length, columns = values_in.shape
    return values_in.astype(jnp.float32).reshape(batch_size, length, columns // HEAD, HEAD)

def attend(queries, keys, values, key_count):
    batch_size, length, columns = queries.shape
    scale = 1.0 / math.sqrt(HEAD)
    scores = jnp.einsum('bqhd,bkhd->bhqk', split_heads(queries), split_heads(keys)) * scale
    visible = jnp.arange(length)[None, None, None, :] < key_count[:, None, None, None]
    scores = jnp.where(visible, scores, MASKED)
    weights = jax.nn.softmax(scores, axis=-1)
    weights_low = weights.astype(jnp.bfloat16)
    context = jnp.einsum('bhqk,bkhd->bqhd', weights_low.astype(jnp.float32), split_heads(values))
    return (context.reshape(batch_size, length, columns).astype(jnp.bfloat16), weights, weights_low)

def attend_back(grad_context, queries, keys, values, weights, weights_low):
    batch_size, length, columns = queries.shape
    scale = 1.0 / math.sqrt(HEAD)
    grad_heads = split_heads(grad_context)
    grad_weights = jnp.einsum('bqhd,bkhd->bhqk', grad_heads, split_heads(values))
    grad_values = jnp.einsum('bhqk,bqhd->bkhd', weights_low.astype(jnp.float32), grad_heads)
    centered = grad_weights - lax.optimization_barrier(jnp.sum(weights * grad_weights, axis=-1, keepdims=True))
    grad_scores = (weights * centered * scale).astype(jnp.bfloat16).astype(jnp.float32)
    grad_queries = jnp.einsum('bhqk,bkhd->bqhd', grad_scores, split_heads(keys))
    grad_keys = jnp.einsum('bhqk,bqhd->bkhd', grad_scores, split_heads(queries))
    shape_out = (batch_size, length, columns)
    return (grad_queries.reshape(shape_out).astype(jnp.bfloat16), grad_keys.reshape(shape_out).astype(jnp.bfloat16), grad_values.reshape(shape_out).astype(jnp.bfloat16))

def norm_back(grad_normed, unit, inverse, gains):
    scaled = grad_normed * gains
    inner = lax.optimization_barrier(jnp.mean(scaled * unit, axis=-1, keepdims=True))
    return inverse * (scaled - unit * inner)

def reference(hidden, gain, w_first, w_second, lengths, cotangent):
    enc_unit, enc_inverse = normalize(hidden[0])
    dec_unit, dec_inverse = normalize(hidden[1])
    memory = (enc_unit * gain[0]).astype(jnp.bfloat16)
    dec_normed = (dec_unit * gain[1]).astype(jnp.bfloat16)
    keys = project(memory, w_first[0]).astype(jnp.bfloat16)
    values = project(memory, w_second[0]).astype(jnp.bfloat16)
    queries = project(dec_normed, w_first[1]).astype(jnp.bfloat16)
    context, weights, weights_low = attend(queries, keys, values, lengths[:, 0])
    output = (hidden[1].astype(jnp.float32) + project_back(context, w_second[1])).astype(jnp.bfloat16)
    keep = jnp.arange(LEN)[None, :] < lengths[:, 1][:, None]
    grad_out = jnp.where(keep[:, :, None], cotangent[1], jnp.zeros((), cotangent.dtype))
    grad_context = project(grad_out, w_second[1]).astype(jnp.bfloat16)
    grad_queries, grad_keys, grad_values = attend_back(grad_context, queries, keys, values, weights, weights_low)
    d_first = jnp.stack([grouped_outer(memory, grad_keys), grouped_outer(dec_normed, grad_queries)])
    d_second = jnp.stack([grouped_outer(memory, grad_values), grouped_outer(grad_out, context)])
    enc_grad = cotangent[0].astype(jnp.float32) + project_back(grad_keys, w_first[0]) + project_back(grad_values, w_second[0])
    dec_grad = project_back(grad_queries, w_first[1])
    d_gain = jnp.stack([grouped_vector(enc_grad * enc_unit), grouped_vector(dec_grad * dec_unit)])
    enc_states = norm_back(enc_grad, enc_unit, enc_inverse, gain[0])
    dec_states = norm_back(dec_grad, dec_unit, dec_inverse, gain[1]) + grad_out.astype(jnp.float32)
    d_hidden = jnp.stack([enc_states, dec_states]).astype(jnp.bfloat16)
    result = jnp.stack([memory, output])
    return (result, d_hidden, d_gain, d_first, d_second)
```

```python
import math

import jax
import jax.numpy as jnp
from jax import lax
from jax.experimental import pallas as pl
from jax.experimental.pallas import tpu as pltpu
from jax.sharding import PartitionSpec as P

HEAD = 128
EPS = 1e-06
MASKED = -1e30
CORES = 2
F32 = jnp.float32
BF16 = jnp.bfloat16


def dot_rows(left, right):
    return lax.dot_general(left, right, (((0,), (0,)), ((), ())), preferred_element_type=F32)


def dot_last(left, right):
    return lax.dot_general(left, right, (((1,), (1,)), ((), ())), preferred_element_type=F32)


def dot_plain(left, right):
    return jnp.dot(left, right, preferred_element_type=F32)


def core_swap(x):
    n = lax.axis_size("dp")
    return lax.ppermute(x, "dp", [(i, i ^ 1) for i in range(n)])


def chip_shift(x, by, decoder_only=False):
    n = lax.axis_size("dp")
    to = [(i + by * CORES) % n for i in range(n)]
    if decoder_only:
        return lax.ppermute(x, ("section", "dp"), [(n + i, n + to[i]) for i in range(n)])
    return lax.ppermute(x, "dp", [(i, to[i]) for i in range(n)])


def head_shift(x, by, decoder_only=False):
    n = lax.axis_size("mp")
    pairs = [(i, (i + by) % n) for i in range(n)]
    if decoder_only:
        return lax.ppermute(x, ("section", "mp"), [(n + i, n + t) for i, t in pairs])
    return lax.ppermute(x, "mp", pairs)


def attention_kernel(lengths_ref, q_ref, k_ref, v_ref, g_ref, ctx_ref, gq_ref, gk_ref, gv_ref):
    scale = 1.0 / math.sqrt(HEAD)
    q, k, v, g = q_ref[...], k_ref[...], v_ref[...], g_ref[...]
    scores = dot_last(q, k) * scale
    column = lax.broadcasted_iota(jnp.int32, scores.shape, 1)
    scores = jnp.where(column < lengths_ref[0, 0], scores, MASKED)
    top = jnp.max(scores, axis=-1, keepdims=True)
    raised = jnp.exp(scores - top)
    weights = raised / jnp.sum(raised, axis=-1, keepdims=True)
    low = weights.astype(BF16)
    ctx_ref[...] = dot_plain(low, v).astype(BF16)
    gv_ref[...] = dot_rows(low, g).astype(BF16)
    grad_weights = dot_last(g, v)
    centered = grad_weights - jnp.sum(weights * grad_weights, axis=-1, keepdims=True)
    grad_scores = (weights * centered * scale).astype(BF16)
    gq_ref[...] = dot_plain(grad_scores, k).astype(BF16)
    gk_ref[...] = dot_rows(grad_scores, q).astype(BF16)


def attention(lengths, q, k, v, g):
    rows, columns = q.shape
    block = pl.BlockSpec((rows, HEAD), lambda h: (0, h))
    shape = jax.ShapeDtypeStruct((rows, columns), BF16)
    heads = columns // HEAD
    return pl.pallas_call(
        attention_kernel,
        grid=(heads,),
        in_specs=[pl.BlockSpec(memory_space=pltpu.SMEM)] + [block] * 4,
        out_specs=[block] * 4,
        out_shape=[shape] * 4,
        compiler_params=pltpu.CompilerParams(vmem_limit_bytes=32 * 2**20),
        cost_estimate=pl.CostEstimate(
            flops=14 * rows * rows * columns,
            bytes_accessed=16 * rows * columns,
            transcendentals=heads * rows * rows,
        ),
        name="attention",
    )(lengths, q, k, v, g)


def ring_sum(parts, me, decoder_only):
    n = parts.shape[1]

    def block(i):
        return lax.dynamic_index_in_dim(parts, lax.rem(i, n), 1, False)

    total = block(me + n - 1)
    for step in range(n - 1):
        total = head_shift(total, 1, decoder_only)
        mine = block(me + 2 * n - 2 - step)
        total = total.astype(F32) + mine.astype(F32)
        if step < n - 2:
            total = total.astype(BF16)
    return total


def ring_gather(rows, me, n, decoder_only):
    whole = jnp.zeros((n,) + rows.shape, rows.dtype)
    whole = lax.dynamic_update_index_in_dim(whole, rows, me, 0)
    held = rows
    for step in range(1, n):
        held = head_shift(held, 1, decoder_only)
        whole = lax.dynamic_update_index_in_dim(whole, held, lax.rem(me + n - step, n), 0)
    return whole.reshape(n * rows.shape[0], rows.shape[1])


def shards(hidden, gain, w_first, w_second, lengths, cotangent):
    encoder = lax.axis_index("section") == 0
    place = lax.axis_index("dp")
    chip, core = place // CORES, lax.rem(place, CORES)
    head_place = lax.axis_index("mp")
    heads_axis = lax.axis_size("mp")
    chips = lax.axis_size("dp") // CORES
    states = hidden[0, 0]
    length, width = states.shape
    gains = gain[0][None, :]
    span = width // chips
    tile = w_first.shape[1]
    columns = w_first.shape[2]
    block = length // heads_axis

    def chip_at(k):
        return lax.rem(chip + k, chips)

    def chip_columns(array, k):
        return lax.dynamic_slice_in_dim(array, chip_at(k) * span, span, 1)

    first, second = w_first[0], w_second[0]

    def whole_chip(own):
        other = core_swap(own)
        return jnp.concatenate(
            [jnp.where(core == 0, own, other), jnp.where(core == 0, other, own)], axis=0
        )

    wide = states.astype(F32)
    inverse = lax.rsqrt(jnp.mean(wide * wide, axis=-1, keepdims=True) + EPS)
    unit = wide * inverse
    normed = (unit * gains).astype(BF16)
    keep = jnp.arange(length)[:, None] < lengths[0, 1]
    grad_out = jnp.where(keep, cotangent[0, 0], jnp.zeros((), BF16))

    left = [chip_columns(normed, 0)]
    left += [chip_shift(chip_columns(normed, k), k) for k in range(1, chips)]
    upper = [chip_columns(grad_out, 0)]
    upper += [chip_shift(chip_columns(grad_out, k), k, True) for k in range(1, chips)]
    first_chip = whole_chip(first)
    second_chip = whole_chip(second)
    right = [jnp.where(encoder, left[k], upper[k]) for k in range(chips)]

    def project(rows, weight):
        parts = [dot_plain(rows[k], weight) for k in range(chips)]
        total = parts[0]
        for k in range(1, chips):
            total = total + chip_shift(parts[k].astype(BF16), -k).astype(F32)
        return total.astype(BF16)

    first_proj = project(left, first_chip)
    second_proj = project(right, second_chip)
    keys = lax.ppermute(first_proj, "section", [(0, 1)])
    values = lax.ppermute(second_proj, "section", [(0, 1)])
    context, grad_query, grad_key, grad_value = attention(
        lengths, first_proj, keys, values, second_proj
    )
    back_value = lax.ppermute(grad_value, "section", [(1, 0)])
    back_key = lax.ppermute(grad_key, "section", [(1, 0)])
    grad_second = jnp.where(encoder, back_value, context)
    grad_first = jnp.where(encoder, back_key, grad_query)
    grads_second = [grad_second] + [chip_shift(grad_second, k) for k in range(1, chips)]
    grads_first = [grad_first] + [chip_shift(grad_first, k) for k in range(1, chips)]

    split = (chips, heads_axis, block, span)
    part_second = jnp.stack([dot_last(g, second_chip) for g in grads_second])
    part_first = jnp.stack([dot_last(g, first_chip) for g in grads_first])
    out_parts = part_second.astype(BF16).reshape(split)
    back_parts = (part_first + jnp.where(encoder, part_second, 0.0)).astype(BF16).reshape(split)

    def full_rows(sums, decoder_only):
        whole = jnp.zeros((block, width), F32)
        whole = lax.dynamic_update_slice_in_dim(whole, sums[0], chip * span, 1)
        for k in range(1, chips):
            got = chip_shift(sums[k].astype(BF16), -k, decoder_only).astype(F32)
            whole = lax.dynamic_update_slice_in_dim(whole, got, chip_at(k) * span, 1)
        return whole

    def my_rows(array):
        return lax.dynamic_slice_in_dim(array, head_place * block, block, 0)

    out_rows = full_rows(ring_sum(out_parts, head_place, True), True)
    out_rows = (my_rows(states).astype(F32) + out_rows).astype(BF16)
    output = ring_gather(out_rows, head_place, heads_axis, True)
    result = jnp.where(encoder, normed, output)

    grad_normed = full_rows(ring_sum(back_parts, head_place, False), False)
    grad_normed = grad_normed + jnp.where(encoder, my_rows(cotangent[0, 0]).astype(F32), 0.0)
    my_inverse = my_rows(inverse)
    my_unit = my_rows(states).astype(F32) * my_inverse
    residual = jnp.where(encoder, 0.0, my_rows(grad_out).astype(F32))
    scaled = grad_normed * gains
    inner = jnp.mean(scaled * my_unit, axis=-1, keepdims=True)
    grad_rows = (my_inverse * (scaled - my_unit * inner) + residual).astype(BF16)
    grad_states = ring_gather(grad_rows, head_place, heads_axis, False)

    gain_part = jnp.sum(grad_normed * my_unit, axis=0, keepdims=True)
    gain_chip = chip_columns(gain_part, 0)
    for k in range(1, chips):
        gain_chip = gain_chip + chip_shift(chip_columns(gain_part, k), k)
    gain_mine = lax.dynamic_slice_in_dim(gain_chip, core * tile, tile, 1)
    gain_mine = gain_mine + core_swap(
        lax.dynamic_slice_in_dim(gain_chip, (1 - core) * tile, tile, 1)
    )
    gain_sum = gain_mine
    for k in range(1, heads_axis):
        gain_sum = gain_sum + head_shift(gain_mine, k)

    def weight_grad(rows, grads):
        rows, grads = jnp.concatenate(rows, axis=0), jnp.concatenate(grads, axis=0)
        own = dot_rows(lax.dynamic_slice_in_dim(rows, core * tile, tile, 1), grads)
        other = dot_rows(lax.dynamic_slice_in_dim(rows, (1 - core) * tile, tile, 1), grads)
        return own + core_swap(other.astype(BF16)).astype(F32)

    first_sum = weight_grad(left, grads_first)
    second_sum = weight_grad(right, grads_second)
    return (
        result[None, None],
        grad_states[None, None],
        gain_sum,
        first_sum[None],
        second_sum[None],
    )


def solution(mesh):
    return jax.shard_map(
        shards,
        mesh=mesh,
        in_specs=(
            P("section", "dp", None, None),
            P("section", None),
            P("section", "dp", "mp"),
            P("section", "dp", "mp"),
            P("dp", None),
            P("section", "dp", None, None),
        ),
        out_specs=(
            P("section", "dp", None, None),
            P("section", "dp", None, None),
            P("section", "dp"),
            P("section", "dp", "mp"),
            P("section", "dp", "mp"),
        ),
        check_vma=False,
    )
```

```python
import math

import jax
import jax.numpy as jnp
from jax import lax
from jax.experimental import pallas as pl
from jax.experimental.pallas import tpu as pltpu
from jax.sharding import PartitionSpec as P

HEAD = 128
EPS = 1e-06
MASKED = -1e30
CORES = 2
F32 = jnp.float32
BF16 = jnp.bfloat16


def dot_rows(left, right):
    return lax.dot_general(left, right, (((0,), (0,)), ((), ())), preferred_element_type=F32)


def dot_last(left, right):
    return lax.dot_general(left, right, (((1,), (1,)), ((), ())), preferred_element_type=F32)


def dot_plain(left, right):
    return jnp.dot(left, right, preferred_element_type=F32)


BOTH, ENCODER, DECODER = (0, 1), (0,), (1,)


def permute(x, axis, to, sections):
    n = lax.axis_size(axis)
    if sections == BOTH:
        return lax.ppermute(x, axis, [(i, to(i, n)) for i in range(n)])
    pairs = [(s * n + i, s * n + to(i, n)) for s in sections for i in range(n)]
    return lax.ppermute(x, ("section", axis), pairs)


def core_swap(x, sections=BOTH):
    return permute(x, "dp", lambda i, n: i ^ 1, sections)


def chip_shift(x, by, sections=BOTH):
    return permute(x, "dp", lambda i, n: (i + by * CORES) % n, sections)


def home_shift(x, by):
    n = lax.axis_size("dp")
    pairs = [(n + i, (i + by * CORES) % n) for i in range(n)]
    return lax.ppermute(x, ("section", "dp"), pairs)


def head_shift(x, by, sections=BOTH):
    return permute(x, "mp", lambda i, n: (i + by) % n, sections)


def after(x, *before):
    return lax.optimization_barrier((x,) + before)[0]


def attention_kernel(lengths_ref, q_ref, kv_ref, g_ref, ctx_ref, gq_ref, gkv_ref):
    scale = 1.0 / math.sqrt(HEAD)
    q, k, v, g = q_ref[...], kv_ref[0], kv_ref[1], g_ref[...]
    scores = dot_last(q, k) * scale
    column = lax.broadcasted_iota(jnp.int32, scores.shape, 1)
    scores = jnp.where(column < lengths_ref[0, 0], scores, MASKED)
    top = jnp.max(scores, axis=-1, keepdims=True)
    raised = jnp.exp(scores - top)
    weights = raised / jnp.sum(raised, axis=-1, keepdims=True)
    low = weights.astype(BF16)
    ctx_ref[...] = dot_plain(low, v).astype(BF16)
    gkv_ref[1] = dot_rows(low, g).astype(BF16)
    grad_weights = dot_last(g, v)
    centered = grad_weights - jnp.sum(weights * grad_weights, axis=-1, keepdims=True)
    grad_scores = (weights * centered * scale).astype(BF16)
    gq_ref[...] = dot_plain(grad_scores, k).astype(BF16)
    gkv_ref[0] = dot_rows(grad_scores, q).astype(BF16)


def attention(lengths, q, kv, g):
    rows, columns = q.shape
    block = pl.BlockSpec((rows, HEAD), lambda h: (0, h))
    pair = pl.BlockSpec((2, rows, HEAD), lambda h: (0, 0, h))
    shape = jax.ShapeDtypeStruct((rows, columns), BF16)
    heads = columns // HEAD
    return pl.pallas_call(
        attention_kernel,
        grid=(heads,),
        in_specs=[pl.BlockSpec(memory_space=pltpu.SMEM), block, pair, block],
        out_specs=[block, block, pair],
        out_shape=[shape, shape, jax.ShapeDtypeStruct((2, rows, columns), BF16)],
        compiler_params=pltpu.CompilerParams(vmem_limit_bytes=32 * 2**20),
        cost_estimate=pl.CostEstimate(
            flops=14 * rows * rows * columns,
            bytes_accessed=16 * rows * columns,
            transcendentals=heads * rows * rows,
        ),
        name="attention",
    )(lengths, q, kv, g)


def shards(hidden, gain, w_first, w_second, lengths, cotangent):
    encoder = lax.axis_index("section") == 0
    place = lax.axis_index("dp")
    chip, core = place // CORES, lax.rem(place, CORES)
    head_place = lax.axis_index("mp")
    heads_axis = lax.axis_size("mp")
    chips = lax.axis_size("dp") // CORES
    states = hidden[0, 0]
    length, width = states.shape
    gains = gain[0][None, :]
    tile = w_first.shape[1]
    span = CORES * tile
    columns = w_first.shape[2]
    block = length // heads_axis
    others = range(1, chips)

    def chip_at(k):
        return lax.rem(chip + k + chips, chips)

    def chip_columns(array, k):
        return lax.dynamic_slice_in_dim(array, chip_at(k) * span, span, 1)

    def in_order(own, other):
        return jnp.concatenate(
            [jnp.where(core == 0, own, other), jnp.where(core == 0, other, own)], axis=0
        )

    def whole_chip(own):
        return in_order(own, core_swap(own))

    first, second = w_first[0], w_second[0]
    cut = tile // 4
    first_far = [chip_shift(first, k, DECODER) for k in others]
    second_upper = [chip_shift(second[:cut], k, DECODER) for k in others]
    far_states = [chip_shift(chip_columns(states, k), k, ENCODER) for k in others]
    first_chip = whole_chip(first)
    second_chip = whole_chip(second)
    wide = states.astype(F32)
    inverse = lax.rsqrt(jnp.mean(wide * wide, axis=-1, keepdims=True) + EPS)
    inverse_row = inverse.reshape(1, length)
    far_inverse = [chip_shift(inverse_row, k, ENCODER).reshape(length, 1) for k in others]
    unit = wide * inverse
    normed = (unit * gains).astype(BF16)
    keep = jnp.arange(length)[:, None] < lengths[0, 1]
    grad_out = jnp.where(keep, cotangent[0, 0], jnp.zeros((), BF16))

    near_normed = chip_columns(normed, 0)
    second_left = jnp.where(encoder, near_normed, chip_columns(grad_out, 0))
    own_first = dot_plain(near_normed, first_chip)
    own_second = dot_plain(second_left, second_chip)
    normed_columns = [chip_columns(normed, -k) for k in others]
    grad_columns = [chip_columns(grad_out, -k) for k in others]
    far_states, own_first, own_second, normed_columns, grad_columns = lax.optimization_barrier(
        (far_states, own_first, own_second, normed_columns, grad_columns)
    )
    gains_chip = chip_columns(gains, 0)
    far_normed = [
        (rows.astype(F32) * inv * gains_chip).astype(BF16)
        for rows, inv in zip(far_states, far_inverse)
    ]

    both = jnp.stack([own_first, own_second])
    for k in others:
        part = jnp.stack(
            [dot_plain(far_normed[k - 1], w).astype(BF16) for w in (first_chip, second_chip)]
        )
        both = both + chip_shift(part, -k, ENCODER).astype(F32)
    both, first_far, second_upper = lax.optimization_barrier(
        (both.astype(BF16), first_far, second_upper)
    )
    second_lower = [
        chip_shift(after(second[cut:], *second_upper), k, DECODER) for k in others
    ]
    memory_heads = lax.ppermute(both, "section", [(0, 1)])

    first_far = [whole_chip(w) for w in first_far]
    queries, grad_context = own_first, own_second
    for k in others:
        queries = queries + dot_plain(normed_columns[k - 1], first_far[k - 1])
    queries = queries.astype(BF16)
    upper_swapped = [core_swap(w) for w in second_upper]
    memory_heads, second_lower, queries, upper_swapped = lax.optimization_barrier(
        (memory_heads, second_lower, queries, upper_swapped)
    )
    second_far = [
        in_order(
            jnp.concatenate([second_upper[i], second_lower[i]], axis=0),
            jnp.concatenate([upper_swapped[i], core_swap(second_lower[i])], axis=0),
        )
        for i in range(chips - 1)
    ]
    for k in others:
        grad_context = grad_context + dot_plain(grad_columns[k - 1], second_far[k - 1])
    context, grad_query, grad_memory = attention(
        lengths, queries, memory_heads, grad_context.astype(BF16)
    )
    grad_memory, *far_memory = [home_shift(grad_memory, k) for k in range(chips)]

    def block_at(array, place):
        at = lax.rem(place + 2 * heads_axis, heads_axis) * block
        return lax.dynamic_slice_in_dim(array, at, block, array.ndim - 2)

    def first_block(parts):
        return block_at(parts, head_place - 1)

    def summed(got, parts, step):
        return got.astype(F32) + block_at(parts, head_place - 2 - step).astype(F32)

    def my_rows(array):
        return block_at(array, head_place)

    def place_rows(whole, rows, step, column=0):
        at = lax.rem(head_place - step + heads_axis, heads_axis) * block
        return lax.dynamic_update_slice(whole, rows, (at, column))

    def piled(parts):
        return jnp.stack([p.astype(BF16) for p in parts])

    last = heads_axis - 1
    out_parts = piled(dot_last(context, w) for w in [second_chip] + second_far)
    grad_query_later = after(grad_query, out_parts)
    back_parts = piled(dot_last(grad_query_later, w) for w in [first_chip] + first_far)

    def send_out(x):
        return head_shift(x, 1, DECODER)

    def send_memory(x):
        return head_shift(x, 1, ENCODER)

    out_held, back_held = first_block(out_parts), first_block(back_parts)
    out_got, back_got = send_out(out_held), send_out(back_held)
    for step in range(last):
        out_sum = summed(after(out_got, back_held), out_parts, step)
        out_held = out_sum.astype(BF16)
        if step < last - 1:
            out_got = send_out(out_held)
        back_sum = summed(after(back_got, out_held), back_parts, step)
        back_held = back_sum.astype(BF16)
        if step < last - 1:
            back_got = send_out(back_held)
        if step == 0:
            round_done = out_held
            memory_parts = piled(
                dot_last(g[0], first_chip) + dot_last(g[1], second_chip)
                for g in [after(grad_memory, back_held)] + far_memory
            )
            memory_held = first_block(memory_parts)
            memory_got = send_memory(memory_held)
        else:
            memory_sum = summed(after(memory_got, back_held), memory_parts, step - 1)
            memory_held = memory_sum.astype(BF16)
            memory_got = send_memory(memory_held)
    memory_sum = summed(memory_got, memory_parts, last - 1)

    def whole_rows(pieces):
        whole = jnp.zeros((block, width), F32)
        for k in range(chips):
            whole = lax.dynamic_update_slice_in_dim(whole, pieces[k], chip_at(-k) * span, 1)
        return whole

    out_rows = (my_rows(states).astype(F32) + whole_rows(out_sum)).astype(BF16)
    homes = [chip_shift(memory_sum[k].astype(BF16), -k, ENCODER).astype(F32) for k in others]
    grad_normed = whole_rows(
        [jnp.where(encoder, memory_sum[0], back_sum[0])]
        + [jnp.where(encoder, homes[chips - 1 - k], back_sum[k]) for k in others]
    )
    grad_normed = grad_normed + jnp.where(encoder, my_rows(cotangent[0, 0]).astype(F32), 0.0)
    my_inverse = my_rows(inverse)
    my_unit = my_rows(states).astype(F32) * my_inverse
    residual = jnp.where(encoder, 0.0, my_rows(grad_out).astype(F32))
    scaled = grad_normed * gains
    inner = jnp.mean(scaled * my_unit, axis=-1, keepdims=True)
    grad_rows = (my_inverse * (scaled - my_unit * inner) + residual).astype(BF16)

    output = place_rows(jnp.zeros((length, width), BF16), out_rows, 0)
    grad_states = place_rows(jnp.zeros((length, width), BF16), grad_rows, 0)
    out_held, back_held = out_rows, grad_rows
    out_got = head_shift(out_held, 1, DECODER)
    back_got = head_shift(back_held, 1)
    for step in range(1, last + 1):
        out_held = after(out_got, back_held)
        output = place_rows(output, out_held, step)
        if step < last:
            out_got = head_shift(out_held, 1, DECODER)
        back_held = after(back_got, out_held)
        grad_states = place_rows(grad_states, back_held, step)
        if step == 1:
            first_arrival = back_held
        if step < last:
            back_got = head_shift(back_held, 1)
    result = jnp.where(encoder, normed, output)

    gain_part = jnp.sum(grad_normed * my_unit, axis=0, keepdims=True)
    gain_parts = [head_shift(gain_part, k) for k in range(1, heads_axis)]
    gain_parts = after(gain_parts, first_arrival)
    for part in gain_parts:
        gain_part = gain_part + part
    gain_chip = chip_columns(gain_part, 0)
    for k in others:
        gain_chip = gain_chip + chip_shift(chip_columns(gain_part, k), k)
    gain_sum = lax.dynamic_slice_in_dim(gain_chip, core * tile, tile, 1)
    gain_sum = gain_sum + core_swap(
        lax.dynamic_slice_in_dim(gain_chip, (1 - core) * tile, tile, 1)
    )

    left, right = [near_normed], [second_left]
    grads_first = [jnp.where(encoder, grad_memory[0], grad_query)]
    grads_second = [jnp.where(encoder, grad_memory[1], context)]
    for k in others:
        moved = chip_shift(after(chip_columns(normed, k), round_done), k, DECODER)
        left.append(jnp.where(encoder, far_normed[k - 1], moved))
        moved = chip_shift(after(chip_columns(grad_out, k), round_done), k, DECODER)
        right.append(jnp.where(encoder, far_normed[k - 1], moved))
        moved = chip_shift(after(grad_query, round_done), k, DECODER)
        grads_first.append(jnp.where(encoder, far_memory[k - 1][0], moved))
        moved = chip_shift(after(context, round_done), k, DECODER)
        grads_second.append(jnp.where(encoder, far_memory[k - 1][1], moved))

    def weight_grad(rows, grads):
        rows, grads = jnp.concatenate(rows, axis=0), jnp.concatenate(grads, axis=0)
        own = dot_rows(lax.dynamic_slice_in_dim(rows, core * tile, tile, 1), grads)
        other = dot_rows(lax.dynamic_slice_in_dim(rows, (1 - core) * tile, tile, 1), grads)
        return own + core_swap(other.astype(BF16)).astype(F32)

    first_sum = weight_grad(left, grads_first)
    second_sum = weight_grad(right, grads_second)
    return (
        result[None, None],
        grad_states[None, None],
        gain_sum,
        first_sum[None],
        second_sum[None],
    )


def solution(mesh):
    return jax.shard_map(
        shards,
        mesh=mesh,
        in_specs=(
            P("section", "dp", None, None),
            P("section", None),
            P("section", "dp", "mp"),
            P("section", "dp", "mp"),
            P("dp", None),
            P("section", "dp", None, None),
        ),
        out_specs=(
            P("section", "dp", None, None),
            P("section", "dp", None, None),
            P("section", "dp"),
            P("section", "dp", "mp"),
            P("section", "dp", "mp"),
        ),
        check_vma=False,
    )
```

```python
import functools
import math

import jax
import jax.numpy as jnp
from jax import lax
from jax.experimental import pallas as pl
from jax.experimental.pallas import tpu as pltpu
from jax.sharding import PartitionSpec as P

HEAD = 128
EPS = 1e-06
MASKED = -1e30
WAIT = 12 * 10**9
CORES = 2
F32 = jnp.float32
BF16 = jnp.bfloat16


def dot_rows(left, right):
    return lax.dot_general(left, right, (((0,), (0,)), ((), ())), preferred_element_type=F32)


def dot_last(left, right):
    return lax.dot_general(left, right, (((1,), (1,)), ((), ())), preferred_element_type=F32)


def dot_plain(left, right):
    return jnp.dot(left, right, preferred_element_type=F32)


BOTH, ENCODER, DECODER = (0, 1), (0,), (1,)


def permute(x, axis, to, sections):
    n = lax.axis_size(axis)
    if sections == BOTH:
        return lax.ppermute(x, axis, [(i, to(i, n)) for i in range(n)])
    pairs = [(s * n + i, s * n + to(i, n)) for s in sections for i in range(n)]
    return lax.ppermute(x, ("section", axis), pairs)


def core_swap(x, sections=BOTH):
    return permute(x, "dp", lambda i, n: i ^ 1, sections)


def chip_shift(x, by, sections=BOTH):
    return permute(x, "dp", lambda i, n: (i + by * CORES) % n, sections)


def home_shift(x, by):
    n = lax.axis_size("dp")
    pairs = [(n + i, (i + by * CORES) % n) for i in range(n)]
    return lax.ppermute(x, ("section", "dp"), pairs)


def head_shift(x, by, sections=BOTH):
    return permute(x, "mp", lambda i, n: (i + by) % n, sections)


ANYWHERE = pl.BlockSpec(memory_space=pl.ANY)


def add_kernel(place_ref, got_ref, part_ref, *refs):
    refs[-1][...] = (got_ref[...].astype(F32) + part_ref[...].astype(F32)).astype(refs[-1].dtype)


def add_block(got, parts, place, dtype, *before):
    seqs, tokens, features = got.shape
    steps = 2 if features % 256 == 0 else 1
    piece = features // steps
    block = pl.BlockSpec((seqs, tokens, piece), lambda i, at: (0, 0, i))
    return pl.pallas_call(
        add_kernel,
        grid_spec=pltpu.PrefetchScalarGridSpec(
            num_scalar_prefetch=1,
            grid=(steps,),
            in_specs=[
                block,
                pl.BlockSpec((seqs, tokens, piece), lambda i, at: (0, at[0], i)),
            ]
            + [ANYWHERE] * len(before),
            out_specs=block,
        ),
        out_shape=jax.ShapeDtypeStruct(got.shape, dtype),
        compiler_params=pltpu.CompilerParams(vmem_limit_bytes=32 * 2**20),
        cost_estimate=pl.CostEstimate(flops=WAIT, bytes_accessed=0, transcendentals=0),
        name="add_block",
    )(place.reshape(1), got, parts, *before)


def place_kernel(place_ref, rows_ref, block_ref, whole_ref, *refs):
    wanted = place_ref[1] == 1
    refs[-1][...] = jnp.where(wanted, rows_ref[...], block_ref[...])


def place_block(whole, rows, place, wanted, *before):
    tokens, features = rows.shape
    steps = 2 if features % 256 == 0 else 1
    piece = features // steps
    where = jnp.stack([place, jnp.int32(1) if wanted is None else wanted.astype(jnp.int32)])
    block = pl.BlockSpec((tokens, piece), lambda i, at: (at[0], i))
    return pl.pallas_call(
        place_kernel,
        grid_spec=pltpu.PrefetchScalarGridSpec(
            num_scalar_prefetch=1,
            grid=(steps,),
            in_specs=[pl.BlockSpec((tokens, piece), lambda i, at: (0, i)), block]
            + [ANYWHERE] * (1 + len(before)),
            out_specs=block,
        ),
        out_shape=jax.ShapeDtypeStruct(whole.shape, whole.dtype),
        input_output_aliases={3: 0},
        compiler_params=pltpu.CompilerParams(vmem_limit_bytes=32 * 2**20),
        cost_estimate=pl.CostEstimate(flops=WAIT, bytes_accessed=0, transcendentals=0),
        name="place_block",
    )(where, rows, whole, whole, *before)


def join_kernel(count, *refs):
    at = 0
    for ref in refs[:count]:
        refs[-1][:, at : at + ref.shape[1]] = ref[...]
        at += ref.shape[1]


def join(parts, *before):
    rows = parts[0].shape[0]
    steps = 2 if rows % 32 == 0 else 1
    width = sum(p.shape[1] for p in parts)

    def block(columns):
        return pl.BlockSpec((rows // steps, columns), lambda i: (i, 0))

    return pl.pallas_call(
        functools.partial(join_kernel, len(parts)),
        grid=(steps,),
        in_specs=[block(p.shape[1]) for p in parts] + [ANYWHERE] * len(before),
        out_specs=block(width),
        out_shape=jax.ShapeDtypeStruct((rows, width), parts[0].dtype),
        compiler_params=pltpu.CompilerParams(vmem_limit_bytes=32 * 2**20),
        cost_estimate=pl.CostEstimate(flops=10**9, bytes_accessed=0, transcendentals=0),
        name="join",
    )(*parts, *before)


def attention_kernel(lengths_ref, q_ref, kv_ref, g_ref, ctx_ref, gq_ref, gkv_ref):
    scale = 1.0 / math.sqrt(HEAD)
    q, k, v, g = q_ref[...], kv_ref[0], kv_ref[1], g_ref[...]
    scores = dot_last(q, k) * scale
    column = lax.broadcasted_iota(jnp.int32, scores.shape, 1)
    scores = jnp.where(column < lengths_ref[0, 0], scores, MASKED)
    top = jnp.max(scores, axis=-1, keepdims=True)
    raised = jnp.exp(scores - top)
    weights = raised / jnp.sum(raised, axis=-1, keepdims=True)
    low = weights.astype(BF16)
    ctx_ref[...] = dot_plain(low, v).astype(BF16)
    gkv_ref[1] = dot_rows(low, g).astype(BF16)
    grad_weights = dot_last(g, v)
    centered = grad_weights - jnp.sum(weights * grad_weights, axis=-1, keepdims=True)
    grad_scores = (weights * centered * scale).astype(BF16)
    gq_ref[...] = dot_plain(grad_scores, k).astype(BF16)
    gkv_ref[0] = dot_rows(grad_scores, q).astype(BF16)


def attention(lengths, q, kv, g):
    rows, columns = q.shape
    block = pl.BlockSpec((rows, HEAD), lambda h: (0, h))
    pair = pl.BlockSpec((2, rows, HEAD), lambda h: (0, 0, h))
    shape = jax.ShapeDtypeStruct((rows, columns), BF16)
    heads = columns // HEAD
    return pl.pallas_call(
        attention_kernel,
        grid=(heads,),
        in_specs=[pl.BlockSpec(memory_space=pltpu.SMEM), block, pair, block],
        out_specs=[block, block, pair],
        out_shape=[shape, shape, jax.ShapeDtypeStruct((2, rows, columns), BF16)],
        compiler_params=pltpu.CompilerParams(vmem_limit_bytes=32 * 2**20),
        cost_estimate=pl.CostEstimate(
            flops=14 * rows * rows * columns,
            bytes_accessed=16 * rows * columns,
            transcendentals=heads * rows * rows,
        ),
        name="attention",
    )(lengths, q, kv, g)


def shards(hidden, gain, w_first, w_second, lengths, cotangent):
    encoder = lax.axis_index("section") == 0
    place = lax.axis_index("dp")
    chip, core = place // CORES, lax.rem(place, CORES)
    head_place = lax.axis_index("mp")
    heads_axis = lax.axis_size("mp")
    chips = lax.axis_size("dp") // CORES
    states = hidden[0, 0]
    length, width = states.shape
    gains = gain[0][None, :]
    tile = w_first.shape[1]
    span = CORES * tile
    columns = w_first.shape[2]
    block = length // heads_axis
    others = range(1, chips)

    def chip_at(k):
        return lax.rem(chip + k + chips, chips)

    def chip_columns(array, k):
        return lax.dynamic_slice_in_dim(array, chip_at(k) * span, span, 1)

    def in_order(own, other):
        ahead = [jnp.where(core == 0, a, b) for a, b in zip(own, other)]
        behind = [jnp.where(core == 0, b, a) for a, b in zip(own, other)]
        return jnp.concatenate(ahead + behind, axis=0)

    def whole_chip(own):
        return in_order([own], [core_swap(own)])

    first, second = w_first[0], w_second[0]
    cut = tile // 4
    first_far = [chip_shift(first, k, DECODER) for k in others]
    second_upper = [chip_shift(second[:cut], k, DECODER) for k in others]
    far_states = [chip_shift(chip_columns(states, k), k, ENCODER) for k in others]
    first_chip = whole_chip(first)
    second_chip = whole_chip(second)
    wide = states.astype(F32)
    inverse = lax.rsqrt(jnp.mean(wide * wide, axis=-1, keepdims=True) + EPS)
    inverse_row = inverse.reshape(1, length)
    far_inverse = [chip_shift(inverse_row, k, ENCODER).reshape(length, 1) for k in others]
    unit = wide * inverse
    normed = (unit * gains).astype(BF16)
    keep = jnp.arange(length)[:, None] < lengths[0, 1]
    grad_out = jnp.where(keep, cotangent[0, 0], jnp.zeros((), BF16))

    near_normed = chip_columns(normed, 0)
    second_left = jnp.where(encoder, near_normed, chip_columns(grad_out, 0))
    own_first = dot_plain(near_normed, first_chip)
    own_second = dot_plain(second_left, second_chip)
    normed_columns = [chip_columns(normed, -k) for k in others]
    grad_columns = [chip_columns(grad_out, -k) for k in others]
    far_states, own_first, own_second, normed_columns, grad_columns = lax.optimization_barrier(
        (far_states, own_first, own_second, normed_columns, grad_columns)
    )
    gains_chip = chip_columns(gains, 0)
    far_normed = [
        (rows.astype(F32) * inv * gains_chip).astype(BF16)
        for rows, inv in zip(far_states, far_inverse)
    ]

    both = jnp.stack([own_first, own_second])
    for k in others:
        part = jnp.stack(
            [dot_plain(far_normed[k - 1], w).astype(BF16) for w in (first_chip, second_chip)]
        )
        both = both + chip_shift(part, -k, ENCODER).astype(F32)
    both, first_far, second_upper = lax.optimization_barrier(
        (both.astype(BF16), first_far, second_upper)
    )
    second_lower = [
        chip_shift(second[cut:], k, DECODER) for k in others
    ]
    memory_heads = lax.ppermute(both, "section", [(0, 1)])

    first_far = [whole_chip(w) for w in first_far]
    queries, grad_context = own_first, own_second
    for k in others:
        queries = queries + dot_plain(normed_columns[k - 1], first_far[k - 1])
    queries = queries.astype(BF16)
    upper_swapped = [core_swap(w) for w in second_upper]
    memory_heads, second_lower, queries, upper_swapped = lax.optimization_barrier(
        (memory_heads, second_lower, queries, upper_swapped)
    )
    second_far = [
        in_order(
            [second_upper[i], second_lower[i]], [upper_swapped[i], core_swap(second_lower[i])]
        )
        for i in range(chips - 1)
    ]
    for k in others:
        grad_context = grad_context + dot_plain(grad_columns[k - 1], second_far[k - 1])
    grad_context = grad_context.astype(BF16)
    context, grad_query, grad_memory = attention(lengths, queries, memory_heads, grad_context)
    grad_memory, *far_memory = [home_shift(grad_memory, k) for k in range(chips)]

    def block_at(array, place):
        at = lax.rem(place + 2 * heads_axis, heads_axis) * block
        return lax.dynamic_slice_in_dim(array, at, block, array.ndim - 2)

    def first_block(parts):
        return block_at(parts, head_place - 1)

    def summed(got, parts, step):
        return got.astype(F32) + block_at(parts, head_place - 2 - step).astype(F32)

    def my_rows(array):
        return block_at(array, head_place)

    def place_rows(whole, rows, step, column=0):
        at = lax.rem(head_place - step + heads_axis, heads_axis) * block
        return lax.dynamic_update_slice(whole, rows, (at, column))

    def piled(parts):
        return jnp.stack([p.astype(BF16) for p in parts])

    last = heads_axis - 1
    def send_out(x):
        return head_shift(x, 1, DECODER)

    def send_memory(x):
        return head_shift(x, 1, ENCODER)

    def whole_rows(pieces):
        whole = jnp.zeros((block, width), F32)
        for k in range(chips):
            whole = lax.dynamic_update_slice_in_dim(whole, pieces[k], chip_at(-k) * span, 1)
        return whole

    back_parts = piled(dot_last(grad_query, w) for w in [first_chip] + first_far)
    back_held = first_block(back_parts)
    back_got = send_out(back_held)
    out_parts = piled(dot_last(context, w) for w in [second_chip] + second_far)
    out_held = first_block(out_parts)
    out_got = send_out(out_held)
    memory_parts = piled(
        dot_last(g[0], first_chip) + dot_last(g[1], second_chip)
        for g in [grad_memory] + far_memory
    )
    memory_held = first_block(memory_parts)
    memory_got = send_memory(memory_held)

    def at(step):
        return lax.rem(head_place + 2 * heads_axis - step, heads_axis)

    for step in range(last):
        kind = BF16 if step < last - 1 else F32
        back_held = add_block(back_got, back_parts, at(2 + step), kind, out_held)
        if step == 0:
            moved = []
            for k in others:
                parts = [chip_columns(normed, k), chip_columns(grad_out, k), grad_query, context]
                moved.append(chip_shift(join(parts, back_held), k, DECODER))
        if step < last - 1:
            back_got = send_out(back_held)
            out_held = add_block(out_got, out_parts, at(2 + step), kind, back_held)
            out_got = send_out(out_held)
        memory_held = add_block(memory_got, memory_parts, at(2 + step), kind, back_held)
        if step < last - 1:
            memory_got = send_memory(memory_held)
    back_sum, memory_sum = back_held, memory_held

    homes = [chip_shift(memory_sum[k].astype(BF16), -k, ENCODER).astype(F32) for k in others]
    grad_normed = whole_rows(
        [jnp.where(encoder, memory_sum[0], back_sum[0])]
        + [jnp.where(encoder, homes[chips - 1 - k], back_sum[k]) for k in others]
    )
    grad_normed = grad_normed + jnp.where(encoder, my_rows(cotangent[0, 0]).astype(F32), 0.0)
    my_inverse = my_rows(inverse)
    my_unit = my_rows(states).astype(F32) * my_inverse
    residual = jnp.where(encoder, 0.0, my_rows(grad_out).astype(F32))
    scaled = grad_normed * gains
    inner = jnp.mean(scaled * my_unit, axis=-1, keepdims=True)
    grad_rows = (my_inverse * (scaled - my_unit * inner) + residual).astype(BF16)

    back_held = grad_rows
    back_got = head_shift(back_held, 1)
    gain_part = jnp.sum(grad_normed * my_unit, axis=0, keepdims=True)
    gain_parts = [head_shift(gain_part, k) for k in range(1, heads_axis)]
    out_sum = add_block(out_got, out_parts, at(1 + last), F32, back_held)
    out_held = (my_rows(states).astype(F32) + whole_rows(out_sum)).astype(BF16)
    out_got = send_out(out_held)
    arrivals = [(out_held, back_held)]

    grad_states = place_block(jnp.zeros_like(normed), back_held, at(0), None, out_held)
    result = place_block(normed, out_held, at(0), ~encoder, grad_states)

    def next_round(step, back_got, out_got, grad_states, result, first, then):
        arrived = back_got
        if step < last:
            back_got = head_shift(arrived, 1)
        grad_states = place_block(grad_states, arrived, at(step), None, result, *first)
        arrived = out_got
        if step < last:
            out_got = send_out(arrived)
        result = place_block(result, arrived, at(step), ~encoder, grad_states, *then)
        return back_got, out_got, grad_states, result

    back_got, out_got, grad_states, result = next_round(
        1, back_got, out_got, grad_states, result, [], []
    )
    for part in gain_parts:
        gain_part = gain_part + part
    gain_chip = chip_columns(gain_part, 0)
    gain_far = [chip_shift(chip_columns(gain_part, k), k) for k in others]
    left, right = [near_normed], [second_left]
    grads_first = [jnp.where(encoder, grad_memory[0], grad_query)]
    grads_second = [jnp.where(encoder, grad_memory[1], context)]
    for k in others:
        pieces = jnp.split(moved[k - 1], (span, 2 * span, 2 * span + columns), axis=1)
        left.append(jnp.where(encoder, far_normed[k - 1], pieces[0]))
        right.append(jnp.where(encoder, far_normed[k - 1], pieces[1]))
        grads_first.append(jnp.where(encoder, far_memory[k - 1][0], pieces[2]))
        grads_second.append(jnp.where(encoder, far_memory[k - 1][1], pieces[3]))

    def weight_grads(half):
        def one(rows, grads):
            rows, grads = jnp.concatenate(rows, axis=0), jnp.concatenate(grads, axis=0)
            return dot_rows(lax.dynamic_slice_in_dim(rows, half * tile, tile, 1), grads)

        return one(left, grads_first), one(right, grads_second)

    halves = jnp.stack([x.astype(BF16) for x in weight_grads(1 - core)])
    swapped = core_swap(halves)
    for step in range(2, last):
        back_got, out_got, grad_states, result = next_round(
            step, back_got, out_got, grad_states, result, [gain_part], [halves]
        )
    for part in gain_far:
        gain_chip = gain_chip + part
    gain_sum = lax.dynamic_slice_in_dim(gain_chip, core * tile, tile, 1)
    gain_sum = gain_sum + core_swap(
        lax.dynamic_slice_in_dim(gain_chip, (1 - core) * tile, tile, 1)
    )
    first_sum, second_sum = weight_grads(core)
    first_sum = first_sum + swapped[0].astype(F32)
    second_sum = second_sum + swapped[1].astype(F32)
    back_got, out_got, grad_states, result = next_round(
        last, back_got, out_got, grad_states, result, [gain_chip, first_sum], [second_sum]
    )
    return (
        result[None, None],
        grad_states[None, None],
        gain_sum,
        first_sum[None],
        second_sum[None],
    )


def solution(mesh):
    return jax.shard_map(
        shards,
        mesh=mesh,
        in_specs=(
            P("section", "dp", None, None),
            P("section", None),
            P("section", "dp", "mp"),
            P("section", "dp", "mp"),
            P("dp", None),
            P("section", "dp", None, None),
        ),
        out_specs=(
            P("section", "dp", None, None),
            P("section", "dp", None, None),
            P("section", "dp"),
            P("section", "dp", "mp"),
            P("section", "dp", "mp"),
        ),
        check_vma=False,
    )
```

```python
import functools
import math

import jax
import jax.numpy as jnp
from jax import lax
from jax.experimental import pallas as pl
from jax.experimental.pallas import tpu as pltpu
from jax.sharding import PartitionSpec as P

HEAD = 128
EPS = 1e-06
MASKED = -1e30
WAIT = 12 * 10**9
CORES = 2
F32 = jnp.float32
BF16 = jnp.bfloat16


def dot_rows(left, right):
    return lax.dot_general(left, right, (((0,), (0,)), ((), ())), preferred_element_type=F32)


def dot_last(left, right):
    return lax.dot_general(left, right, (((1,), (1,)), ((), ())), preferred_element_type=F32)


def dot_plain(left, right):
    return jnp.dot(left, right, preferred_element_type=F32)


BOTH, ENCODER, DECODER = (0, 1), (0,), (1,)


def permute(x, axis, to, sections):
    n = lax.axis_size(axis)
    if sections == BOTH:
        return lax.ppermute(x, axis, [(i, to(i, n)) for i in range(n)])
    pairs = [(s * n + i, s * n + to(i, n)) for s in sections for i in range(n)]
    return lax.ppermute(x, ("section", axis), pairs)


def core_swap(x, sections=BOTH):
    return permute(x, "dp", lambda i, n: i ^ 1, sections)


def chip_shift(x, by, sections=BOTH):
    return permute(x, "dp", lambda i, n: (i + by * CORES) % n, sections)


def home_shift(x, by):
    n = lax.axis_size("dp")
    pairs = [(n + i, (i + by * CORES) % n) for i in range(n)]
    return lax.ppermute(x, ("section", "dp"), pairs)


def head_shift(x, by, sections=BOTH):
    return permute(x, "mp", lambda i, n: (i + by) % n, sections)


ANYWHERE = pl.BlockSpec(memory_space=pl.ANY)


def add_kernel(place_ref, got_ref, part_ref, *refs):
    refs[-1][...] = (got_ref[...].astype(F32) + part_ref[...].astype(F32)).astype(refs[-1].dtype)


def add_block(got, parts, place, dtype, *before):
    seqs, tokens, features = got.shape
    steps = 2 if features % 256 == 0 else 1
    piece = features // steps
    block = pl.BlockSpec((seqs, tokens, piece), lambda i, at: (0, 0, i))
    return pl.pallas_call(
        add_kernel,
        grid_spec=pltpu.PrefetchScalarGridSpec(
            num_scalar_prefetch=1,
            grid=(steps,),
            in_specs=[
                block,
                pl.BlockSpec((seqs, tokens, piece), lambda i, at: (0, at[0], i)),
            ]
            + [ANYWHERE] * len(before),
            out_specs=block,
        ),
        out_shape=jax.ShapeDtypeStruct(got.shape, dtype),
        compiler_params=pltpu.CompilerParams(vmem_limit_bytes=32 * 2**20),
        cost_estimate=pl.CostEstimate(flops=WAIT, bytes_accessed=0, transcendentals=0),
        name="add_block",
    )(place.reshape(1), got, parts, *before)


def place_kernel(place_ref, rows_ref, other_ref, *refs):
    refs[-1][...] = jnp.where(place_ref[1] == 1, rows_ref[...], other_ref[...])


def place_block(whole, length, rows, place, other, wanted, *before):
    tokens, features = rows.shape
    steps = 2 if features % 256 == 0 else 1
    piece = features // steps
    where = jnp.stack([place, wanted.astype(jnp.int32)])
    block = pl.BlockSpec((tokens, piece), lambda i, at: (at[0], i))
    mine = pl.BlockSpec((tokens, piece), lambda i, at: (0, i))
    whole = [] if whole is None else [whole]
    if other is None:
        other, other_block = rows, mine
    else:
        other_block = block
    return pl.pallas_call(
        place_kernel,
        grid_spec=pltpu.PrefetchScalarGridSpec(
            num_scalar_prefetch=1,
            grid=(steps,),
            in_specs=[mine, other_block] + [ANYWHERE] * len(whole + list(before)),
            out_specs=block,
        ),
        out_shape=jax.ShapeDtypeStruct((length, features), rows.dtype),
        input_output_aliases={3: 0} if whole else {},
        compiler_params=pltpu.CompilerParams(vmem_limit_bytes=32 * 2**20),
        cost_estimate=pl.CostEstimate(flops=WAIT, bytes_accessed=0, transcendentals=0),
        name="place_block",
    )(where, rows, other, *whole, *before)


def pass_kernel(rows_ref, *refs):
    refs[-1][...] = rows_ref[...]


def pass_on(rows, *before):
    block = pl.BlockSpec(rows.shape, lambda i: (0, 0))
    return pl.pallas_call(
        pass_kernel,
        grid=(1,),
        in_specs=[block] + [ANYWHERE] * len(before),
        out_specs=block,
        out_shape=jax.ShapeDtypeStruct(rows.shape, rows.dtype),
        compiler_params=pltpu.CompilerParams(vmem_limit_bytes=32 * 2**20),
        cost_estimate=pl.CostEstimate(flops=10**9, bytes_accessed=0, transcendentals=0),
        name="pass_on",
    )(rows, *before)


def join_kernel(count, *refs):
    at = 0
    for ref in refs[:count]:
        refs[-1][:, at : at + ref.shape[1]] = ref[...]
        at += ref.shape[1]


def join(parts, *before):
    rows = parts[0].shape[0]
    steps = 2 if rows % 32 == 0 else 1
    width = sum(p.shape[1] for p in parts)

    def block(columns):
        return pl.BlockSpec((rows // steps, columns), lambda i: (i, 0))

    return pl.pallas_call(
        functools.partial(join_kernel, len(parts)),
        grid=(steps,),
        in_specs=[block(p.shape[1]) for p in parts] + [ANYWHERE] * len(before),
        out_specs=block(width),
        out_shape=jax.ShapeDtypeStruct((rows, width), parts[0].dtype),
        compiler_params=pltpu.CompilerParams(vmem_limit_bytes=32 * 2**20),
        cost_estimate=pl.CostEstimate(flops=10**9, bytes_accessed=0, transcendentals=0),
        name="join",
    )(*parts, *before)


def attention_kernel(lengths_ref, q_ref, kv_ref, g_ref, ctx_ref, gq_ref, gkv_ref):
    scale = 1.0 / math.sqrt(HEAD)
    q, k, v, g = q_ref[...], kv_ref[0], kv_ref[1], g_ref[...]
    scores = dot_last(q, k) * scale
    column = lax.broadcasted_iota(jnp.int32, scores.shape, 1)
    scores = jnp.where(column < lengths_ref[0, 0], scores, MASKED)
    top = jnp.max(scores, axis=-1, keepdims=True)
    raised = jnp.exp(scores - top)
    weights = raised / jnp.sum(raised, axis=-1, keepdims=True)
    low = weights.astype(BF16)
    ctx_ref[...] = dot_plain(low, v).astype(BF16)
    gkv_ref[1] = dot_rows(low, g).astype(BF16)
    grad_weights = dot_last(g, v)
    centered = grad_weights - jnp.sum(weights * grad_weights, axis=-1, keepdims=True)
    grad_scores = (weights * centered * scale).astype(BF16)
    gq_ref[...] = dot_plain(grad_scores, k).astype(BF16)
    gkv_ref[0] = dot_rows(grad_scores, q).astype(BF16)


def attention(lengths, q, kv, g):
    rows, columns = q.shape
    block = pl.BlockSpec((rows, HEAD), lambda h: (0, h))
    pair = pl.BlockSpec((2, rows, HEAD), lambda h: (0, 0, h))
    shape = jax.ShapeDtypeStruct((rows, columns), BF16)
    heads = columns // HEAD
    return pl.pallas_call(
        attention_kernel,
        grid=(heads,),
        in_specs=[pl.BlockSpec(memory_space=pltpu.SMEM), block, pair, block],
        out_specs=[block, block, pair],
        out_shape=[shape, shape, jax.ShapeDtypeStruct((2, rows, columns), BF16)],
        compiler_params=pltpu.CompilerParams(vmem_limit_bytes=32 * 2**20),
        cost_estimate=pl.CostEstimate(
            flops=14 * rows * rows * columns,
            bytes_accessed=16 * rows * columns,
            transcendentals=heads * rows * rows,
        ),
        name="attention",
    )(lengths, q, kv, g)


def shards(hidden, gain, w_first, w_second, lengths, cotangent):
    encoder = lax.axis_index("section") == 0
    place = lax.axis_index("dp")
    chip, core = place // CORES, lax.rem(place, CORES)
    head_place = lax.axis_index("mp")
    heads_axis = lax.axis_size("mp")
    chips = lax.axis_size("dp") // CORES
    states = hidden[0, 0]
    length, width = states.shape
    gains = gain[0][None, :]
    tile = w_first.shape[1]
    span = CORES * tile
    columns = w_first.shape[2]
    block = length // heads_axis
    others = range(1, chips)

    def chip_at(k):
        return lax.rem(chip + k + chips, chips)

    def chip_columns(array, k):
        return lax.dynamic_slice_in_dim(array, chip_at(k) * span, span, 1)

    def in_order(own, other):
        ahead = [jnp.where(core == 0, a, b) for a, b in zip(own, other)]
        behind = [jnp.where(core == 0, b, a) for a, b in zip(own, other)]
        return jnp.concatenate(ahead + behind, axis=0)

    def whole_chip(own):
        return in_order([own], [core_swap(own)])

    first, second = w_first[0], w_second[0]
    first_far = [chip_shift(first, k, DECODER) for k in others]
    far_states = [chip_shift(chip_columns(states, k), k, ENCODER) for k in others]
    first_chip = whole_chip(first)
    second_chip = whole_chip(second)
    wide = states.astype(F32)
    inverse = lax.rsqrt(jnp.mean(wide * wide, axis=-1, keepdims=True) + EPS)
    inverse_row = inverse.reshape(1, length)
    far_inverse = [chip_shift(inverse_row, k, ENCODER).reshape(length, 1) for k in others]
    unit = wide * inverse
    normed = (unit * gains).astype(BF16)
    keep = jnp.arange(length)[:, None] < lengths[0, 1]
    grad_out = jnp.where(keep, cotangent[0, 0], jnp.zeros((), BF16))

    near_normed = chip_columns(normed, 0)
    second_left = jnp.where(encoder, near_normed, chip_columns(grad_out, 0))
    own_first = dot_plain(near_normed, first_chip)
    own_second = dot_plain(second_left, second_chip)
    normed_columns = [chip_columns(normed, -k) for k in others]
    grad_columns = [chip_columns(grad_out, -k) for k in others]
    far_states, own_first, own_second, normed_columns, grad_columns = lax.optimization_barrier(
        (far_states, own_first, own_second, normed_columns, grad_columns)
    )
    gains_chip = chip_columns(gains, 0)
    far_normed = [
        (rows.astype(F32) * inv * gains_chip).astype(BF16)
        for rows, inv in zip(far_states, far_inverse)
    ]

    both = jnp.stack([own_first, own_second])
    for k in others:
        part = jnp.stack(
            [dot_plain(far_normed[k - 1], w).astype(BF16) for w in (first_chip, second_chip)]
        )
        both = both + chip_shift(part, -k, ENCODER).astype(F32)
    both, first_far = lax.optimization_barrier((both.astype(BF16), first_far))
    second_far = [chip_shift(second, k, DECODER) for k in others]
    memory_heads = lax.ppermute(both, "section", [(0, 1)])

    first_far = [whole_chip(w) for w in first_far]
    queries, grad_context = own_first, own_second
    for k in others:
        queries = queries + dot_plain(normed_columns[k - 1], first_far[k - 1])
    queries = queries.astype(BF16)
    memory_heads, second_far, queries = lax.optimization_barrier(
        (memory_heads, second_far, queries)
    )
    second_far = [whole_chip(w) for w in second_far]
    for k in others:
        grad_context = grad_context + dot_plain(grad_columns[k - 1], second_far[k - 1])
    grad_context = grad_context.astype(BF16)
    context, grad_query, grad_memory = attention(lengths, queries, memory_heads, grad_context)
    grad_memory, *far_memory = [home_shift(grad_memory, k) for k in range(chips)]

    def block_at(array, place):
        at = lax.rem(place + 2 * heads_axis, heads_axis) * block
        return lax.dynamic_slice_in_dim(array, at, block, array.ndim - 2)

    def first_block(parts):
        return block_at(parts, head_place - 1)

    def summed(got, parts, step):
        return got.astype(F32) + block_at(parts, head_place - 2 - step).astype(F32)

    def my_rows(array):
        return block_at(array, head_place)

    def place_rows(whole, rows, step, column=0):
        at = lax.rem(head_place - step + heads_axis, heads_axis) * block
        return lax.dynamic_update_slice(whole, rows, (at, column))

    def piled(parts):
        return jnp.stack([p.astype(BF16) for p in parts])

    last = heads_axis - 1
    def send_out(x):
        return head_shift(x, 1, DECODER)

    def send_memory(x):
        return head_shift(x, 1, ENCODER)

    def whole_rows(pieces):
        whole = jnp.zeros((block, width), F32)
        for k in range(chips):
            whole = lax.dynamic_update_slice_in_dim(whole, pieces[k], chip_at(-k) * span, 1)
        return whole

    back_parts = piled(dot_last(grad_query, w) for w in [first_chip] + first_far)
    back_held = first_block(back_parts)
    back_got = send_out(back_held)
    out_parts = piled(dot_last(context, w) for w in [second_chip] + second_far)
    out_held = first_block(out_parts)
    out_got = send_out(out_held)
    memory_parts = piled(
        dot_last(g[0], first_chip) + dot_last(g[1], second_chip)
        for g in [grad_memory] + far_memory
    )
    memory_held = first_block(memory_parts)
    memory_got = send_memory(memory_held)

    def at(step):
        return lax.rem(head_place + 2 * heads_axis - step, heads_axis)

    for step in range(last):
        kind = BF16 if step < last - 1 else F32
        back_held = add_block(back_got, back_parts, at(2 + step), kind, out_held)
        if step == 0:
            moved = []
            for k in others:
                parts = [chip_columns(normed, k), chip_columns(grad_out, k), grad_query, context]
                moved.append(chip_shift(join(parts, back_held), k, DECODER))
        if step < last - 1:
            back_got = send_out(back_held)
            out_held = add_block(out_got, out_parts, at(2 + step), kind, back_held)
            out_got = send_out(out_held)
        memory_held = add_block(memory_got, memory_parts, at(2 + step), kind, back_held)
        if step < last - 1:
            memory_got = send_memory(memory_held)
    back_sum, memory_sum = back_held, memory_held

    homes = [chip_shift(memory_sum[k].astype(BF16), -k, ENCODER).astype(F32) for k in others]
    grad_normed = whole_rows(
        [jnp.where(encoder, memory_sum[0], back_sum[0])]
        + [jnp.where(encoder, homes[chips - 1 - k], back_sum[k]) for k in others]
    )
    grad_normed = grad_normed + jnp.where(encoder, my_rows(cotangent[0, 0]).astype(F32), 0.0)
    my_inverse = my_rows(inverse)
    my_unit = my_rows(states).astype(F32) * my_inverse
    residual = jnp.where(encoder, 0.0, my_rows(grad_out).astype(F32))
    scaled = grad_normed * gains
    inner = jnp.mean(scaled * my_unit, axis=-1, keepdims=True)
    grad_rows = (my_inverse * (scaled - my_unit * inner) + residual).astype(BF16)

    back_held = grad_rows
    back_got = head_shift(back_held, 1)
    gain_part = jnp.sum(grad_normed * my_unit, axis=0, keepdims=True)
    gain_parts = [head_shift(gain_part, k) for k in range(1, heads_axis)]
    out_sum = add_block(out_got, out_parts, at(1 + last), F32, back_held)
    out_held = (my_rows(states).astype(F32) + whole_rows(out_sum)).astype(BF16)
    out_got = send_out(out_held)
    arrivals = [(out_held, back_held)]

    decoder, always = ~encoder, jnp.bool_(True)

    def place_grad(whole, rows, step, *before):
        return place_block(whole, length, rows, at(step), None, always, *before)

    def place_out(whole, rows, step, *before):
        return place_block(whole, length, rows, at(step), normed, decoder, *before)

    def next_round(step, back_got, out_got, grad_states, result, first, then):
        arrived = back_got
        if step < last:
            back_got = head_shift(arrived, 1)
        grad_states = place_grad(grad_states, arrived, step, result, *first)
        arrived = out_got
        if step < last:
            out_got = send_out(arrived)
        result = place_out(result, arrived, step, grad_states, *then)
        return back_got, out_got, grad_states, result

    arrived = back_got
    back_got = head_shift(arrived, 1)
    grad_states = place_grad(None, arrived, 1, out_held)
    arrived = out_got
    out_got = send_out(arrived)
    result = place_out(None, arrived, 1, grad_states)
    grad_states = place_grad(grad_states, back_held, 0, result)
    result = place_out(result, out_held, 0, grad_states)
    for part in gain_parts:
        gain_part = gain_part + part
    gain_part = pass_on(gain_part, back_got)
    gain_chip = chip_columns(gain_part, 0)
    gain_far = [chip_shift(chip_columns(gain_part, k), k) for k in others]
    left, right = [near_normed], [second_left]
    grads_first = [jnp.where(encoder, grad_memory[0], grad_query)]
    grads_second = [jnp.where(encoder, grad_memory[1], context)]
    for k in others:
        pieces = jnp.split(moved[k - 1], (span, 2 * span, 2 * span + columns), axis=1)
        left.append(jnp.where(encoder, far_normed[k - 1], pieces[0]))
        right.append(jnp.where(encoder, far_normed[k - 1], pieces[1]))
        grads_first.append(jnp.where(encoder, far_memory[k - 1][0], pieces[2]))
        grads_second.append(jnp.where(encoder, far_memory[k - 1][1], pieces[3]))

    def weight_grads(half):
        def one(rows, grads):
            rows, grads = jnp.concatenate(rows, axis=0), jnp.concatenate(grads, axis=0)
            return dot_rows(lax.dynamic_slice_in_dim(rows, half * tile, tile, 1), grads)

        return one(left, grads_first), one(right, grads_second)

    halves = jnp.stack([x.astype(BF16) for x in weight_grads(1 - core)])
    swapped = core_swap(halves)
    for step in range(2, last):
        back_got, out_got, grad_states, result = next_round(
            step, back_got, out_got, grad_states, result, [gain_part], [halves]
        )
    for part in gain_far:
        gain_chip = gain_chip + part
    gain_sum = lax.dynamic_slice_in_dim(gain_chip, core * tile, tile, 1)
    gain_sum = gain_sum + core_swap(
        lax.dynamic_slice_in_dim(gain_chip, (1 - core) * tile, tile, 1)
    )
    first_sum, second_sum = weight_grads(core)
    first_sum = first_sum + swapped[0].astype(F32)
    second_sum = second_sum + swapped[1].astype(F32)
    back_got, out_got, grad_states, result = next_round(
        last, back_got, out_got, grad_states, result, [gain_chip, first_sum], [second_sum]
    )
    return (
        result[None, None],
        grad_states[None, None],
        gain_sum,
        first_sum[None],
        second_sum[None],
    )


def solution(mesh):
    return jax.shard_map(
        shards,
        mesh=mesh,
        in_specs=(
            P("section", "dp", None, None),
            P("section", None),
            P("section", "dp", "mp"),
            P("section", "dp", "mp"),
            P("dp", None),
            P("section", "dp", None, None),
        ),
        out_specs=(
            P("section", "dp", None, None),
            P("section", "dp", None, None),
            P("section", "dp"),
            P("section", "dp", "mp"),
            P("section", "dp", "mp"),
        ),
        check_vma=False,
    )
```

```python
import functools
import math

import jax
import jax.numpy as jnp
from jax import lax
from jax.experimental import pallas as pl
from jax.experimental.pallas import tpu as pltpu
from jax.sharding import PartitionSpec as P

HEAD = 128
EPS = 1e-06
MASKED = -1e30
WAIT = 12 * 10**9
CORES = 2
F32 = jnp.float32
BF16 = jnp.bfloat16


def dot_rows(left, right):
    return lax.dot_general(left, right, (((0,), (0,)), ((), ())), preferred_element_type=F32)


def dot_last(left, right):
    return lax.dot_general(left, right, (((1,), (1,)), ((), ())), preferred_element_type=F32)


def dot_plain(left, right):
    return jnp.dot(left, right, preferred_element_type=F32)


BOTH, ENCODER, DECODER = (0, 1), (0,), (1,)


def permute(x, axis, to, sections):
    n = lax.axis_size(axis)
    if sections == BOTH:
        return lax.ppermute(x, axis, [(i, to(i, n)) for i in range(n)])
    pairs = [(s * n + i, s * n + to(i, n)) for s in sections for i in range(n)]
    return lax.ppermute(x, ("section", axis), pairs)


def core_swap(x, sections=BOTH):
    return permute(x, "dp", lambda i, n: i ^ 1, sections)


def chip_shift(x, by, sections=BOTH):
    return permute(x, "dp", lambda i, n: (i + by * CORES) % n, sections)


def home_shift(x, by):
    n = lax.axis_size("dp")
    pairs = [(n + i, (i + by * CORES) % n) for i in range(n)]
    return lax.ppermute(x, ("section", "dp"), pairs)


def head_shift(x, by, sections=BOTH):
    return permute(x, "mp", lambda i, n: (i + by) % n, sections)


ANYWHERE = pl.BlockSpec(memory_space=pl.ANY)


def add_kernel(place_ref, got_ref, part_ref, *refs):
    refs[-1][...] = (got_ref[...].astype(F32) + part_ref[...].astype(F32)).astype(refs[-1].dtype)


def add_block(got, parts, place, dtype, *before):
    seqs, tokens, features = got.shape
    steps = 2 if features % 256 == 0 else 1
    piece = features // steps
    block = pl.BlockSpec((seqs, tokens, piece), lambda i, at: (0, 0, i))
    return pl.pallas_call(
        add_kernel,
        grid_spec=pltpu.PrefetchScalarGridSpec(
            num_scalar_prefetch=1,
            grid=(steps,),
            in_specs=[
                block,
                pl.BlockSpec((seqs, tokens, piece), lambda i, at: (0, at[0], i)),
            ]
            + [ANYWHERE] * len(before),
            out_specs=block,
        ),
        out_shape=jax.ShapeDtypeStruct(got.shape, dtype),
        compiler_params=pltpu.CompilerParams(vmem_limit_bytes=32 * 2**20),
        cost_estimate=pl.CostEstimate(flops=WAIT, bytes_accessed=0, transcendentals=0),
        name="add_block",
    )(place.reshape(1), got, parts, *before)


def place_kernel(place_ref, rows_ref, other_ref, *refs):
    out_ref, token_ref, ready, sem = refs[-4:]
    token_ref[...] = jnp.zeros_like(token_ref)
    tokens = rows_ref.shape[0]
    at = pl.multiple_of(place_ref[0] * tokens, tokens)
    ready[...] = jnp.where(place_ref[1] == 1, rows_ref[...], other_ref[...])
    copy = pltpu.make_async_copy(ready, out_ref.at[pl.ds(at, tokens)], sem)
    copy.start()
    copy.wait()


def place_block(whole, length, rows, place, other, wanted, *before):
    tokens, features = rows.shape
    where = jnp.stack([place, wanted.astype(jnp.int32)])
    mine = pl.BlockSpec((tokens, features), lambda i, at: (0, 0))
    whole = [] if whole is None else [whole]
    if other is None:
        other, other_block = rows, mine
    else:
        other_block = pl.BlockSpec((tokens, features), lambda i, at: (at[0], 0))
    return pl.pallas_call(
        place_kernel,
        grid_spec=pltpu.PrefetchScalarGridSpec(
            num_scalar_prefetch=1,
            grid=(1,),
            in_specs=[mine, other_block] + [ANYWHERE] * len(whole + list(before)),
            out_specs=[ANYWHERE, pl.BlockSpec((8, 128), lambda i, at: (0, 0))],
            scratch_shapes=[
                pltpu.VMEM((tokens, features), rows.dtype),
                pltpu.SemaphoreType.DMA,
            ],
        ),
        out_shape=[
            jax.ShapeDtypeStruct((length, features), rows.dtype),
            jax.ShapeDtypeStruct((8, 128), F32),
        ],
        input_output_aliases={3: 0} if whole else {},
        compiler_params=pltpu.CompilerParams(vmem_limit_bytes=32 * 2**20),
        cost_estimate=pl.CostEstimate(flops=WAIT, bytes_accessed=0, transcendentals=0),
        name="place_block",
    )(where, rows, other, *whole, *before)


def pass_kernel(rows_ref, *refs):
    refs[-1][...] = rows_ref[...]


def pass_on(rows, *before):
    block = pl.BlockSpec(rows.shape, lambda i: (0, 0))
    return pl.pallas_call(
        pass_kernel,
        grid=(1,),
        in_specs=[block] + [ANYWHERE] * len(before),
        out_specs=block,
        out_shape=jax.ShapeDtypeStruct(rows.shape, rows.dtype),
        compiler_params=pltpu.CompilerParams(vmem_limit_bytes=32 * 2**20),
        cost_estimate=pl.CostEstimate(flops=10**9, bytes_accessed=0, transcendentals=0),
        name="pass_on",
    )(rows, *before)


def join_kernel(count, *refs):
    at = 0
    for ref in refs[:count]:
        refs[-1][:, at : at + ref.shape[1]] = ref[...]
        at += ref.shape[1]


def join(parts, *before):
    rows = parts[0].shape[0]
    steps = 2 if rows % 32 == 0 else 1
    width = sum(p.shape[1] for p in parts)

    def block(columns):
        return pl.BlockSpec((rows // steps, columns), lambda i: (i, 0))

    return pl.pallas_call(
        functools.partial(join_kernel, len(parts)),
        grid=(steps,),
        in_specs=[block(p.shape[1]) for p in parts] + [ANYWHERE] * len(before),
        out_specs=block(width),
        out_shape=jax.ShapeDtypeStruct((rows, width), parts[0].dtype),
        compiler_params=pltpu.CompilerParams(vmem_limit_bytes=32 * 2**20),
        cost_estimate=pl.CostEstimate(flops=10**9, bytes_accessed=0, transcendentals=0),
        name="join",
    )(*parts, *before)


def attention_kernel(lengths_ref, q_ref, kv_ref, g_ref, ctx_ref, gq_ref, gkv_ref):
    scale = 1.0 / math.sqrt(HEAD)
    q, k, v, g = q_ref[...], kv_ref[0], kv_ref[1], g_ref[...]
    scores = dot_last(q, k) * scale
    column = lax.broadcasted_iota(jnp.int32, scores.shape, 1)
    scores = jnp.where(column < lengths_ref[0, 0], scores, MASKED)
    top = jnp.max(scores, axis=-1, keepdims=True)
    raised = jnp.exp(scores - top)
    weights = raised / jnp.sum(raised, axis=-1, keepdims=True)
    low = weights.astype(BF16)
    ctx_ref[...] = dot_plain(low, v).astype(BF16)
    gkv_ref[1] = dot_rows(low, g).astype(BF16)
    grad_weights = dot_last(g, v)
    centered = grad_weights - jnp.sum(weights * grad_weights, axis=-1, keepdims=True)
    grad_scores = (weights * centered * scale).astype(BF16)
    gq_ref[...] = dot_plain(grad_scores, k).astype(BF16)
    gkv_ref[0] = dot_rows(grad_scores, q).astype(BF16)


def attention(lengths, q, kv, g):
    rows, columns = q.shape
    block = pl.BlockSpec((rows, HEAD), lambda h: (0, h))
    pair = pl.BlockSpec((2, rows, HEAD), lambda h: (0, 0, h))
    shape = jax.ShapeDtypeStruct((rows, columns), BF16)
    heads = columns // HEAD
    return pl.pallas_call(
        attention_kernel,
        grid=(heads,),
        in_specs=[pl.BlockSpec(memory_space=pltpu.SMEM), block, pair, block],
        out_specs=[block, block, pair],
        out_shape=[shape, shape, jax.ShapeDtypeStruct((2, rows, columns), BF16)],
        compiler_params=pltpu.CompilerParams(vmem_limit_bytes=32 * 2**20),
        cost_estimate=pl.CostEstimate(
            flops=14 * rows * rows * columns,
            bytes_accessed=16 * rows * columns,
            transcendentals=heads * rows * rows,
        ),
        name="attention",
    )(lengths, q, kv, g)


def shards(hidden, gain, w_first, w_second, lengths, cotangent):
    encoder = lax.axis_index("section") == 0
    place = lax.axis_index("dp")
    chip, core = place // CORES, lax.rem(place, CORES)
    head_place = lax.axis_index("mp")
    heads_axis = lax.axis_size("mp")
    chips = lax.axis_size("dp") // CORES
    states = hidden[0, 0]
    length, width = states.shape
    gains = gain[0][None, :]
    tile = w_first.shape[1]
    span = CORES * tile
    columns = w_first.shape[2]
    block = length // heads_axis
    others = range(1, chips)

    def chip_at(k):
        return lax.rem(chip + k + chips, chips)

    def chip_columns(array, k):
        return lax.dynamic_slice_in_dim(array, chip_at(k) * span, span, 1)

    def in_order(own, other):
        ahead = [jnp.where(core == 0, a, b) for a, b in zip(own, other)]
        behind = [jnp.where(core == 0, b, a) for a, b in zip(own, other)]
        return jnp.concatenate(ahead + behind, axis=0)

    def whole_chip(own):
        return in_order([own], [core_swap(own)])

    first, second = w_first[0], w_second[0]
    first_far = [chip_shift(first, k, DECODER) for k in others]
    far_states = [chip_shift(chip_columns(states, k), k, ENCODER) for k in others]
    first_chip = whole_chip(first)
    second_chip = whole_chip(second)
    wide = states.astype(F32)
    inverse = lax.rsqrt(jnp.mean(wide * wide, axis=-1, keepdims=True) + EPS)
    inverse_row = inverse.reshape(1, length)
    far_inverse = [chip_shift(inverse_row, k, ENCODER).reshape(length, 1) for k in others]
    unit = wide * inverse
    normed = (unit * gains).astype(BF16)
    keep = jnp.arange(length)[:, None] < lengths[0, 1]
    grad_out = jnp.where(keep, cotangent[0, 0], jnp.zeros((), BF16))

    near_normed = chip_columns(normed, 0)
    second_left = jnp.where(encoder, near_normed, chip_columns(grad_out, 0))
    own_first = dot_plain(near_normed, first_chip)
    own_second = dot_plain(second_left, second_chip)
    normed_columns = [chip_columns(normed, -k) for k in others]
    grad_columns = [chip_columns(grad_out, -k) for k in others]
    far_states, own_first, own_second, normed_columns, grad_columns = lax.optimization_barrier(
        (far_states, own_first, own_second, normed_columns, grad_columns)
    )
    gains_chip = chip_columns(gains, 0)
    far_normed = [
        (rows.astype(F32) * inv * gains_chip).astype(BF16)
        for rows, inv in zip(far_states, far_inverse)
    ]

    both = jnp.stack([own_first, own_second])
    for k in others:
        part = jnp.stack(
            [dot_plain(far_normed[k - 1], w).astype(BF16) for w in (first_chip, second_chip)]
        )
        both = both + chip_shift(part, -k, ENCODER).astype(F32)
    both, first_far = lax.optimization_barrier((both.astype(BF16), first_far))
    second_far = [chip_shift(second, k, DECODER) for k in others]
    memory_heads = lax.ppermute(both, "section", [(0, 1)])

    first_far = [whole_chip(w) for w in first_far]
    queries, grad_context = own_first, own_second
    for k in others:
        queries = queries + dot_plain(normed_columns[k - 1], first_far[k - 1])
    queries = queries.astype(BF16)
    memory_heads, second_far, queries = lax.optimization_barrier(
        (memory_heads, second_far, queries)
    )
    second_far = [whole_chip(w) for w in second_far]
    for k in others:
        grad_context = grad_context + dot_plain(grad_columns[k - 1], second_far[k - 1])
    grad_context = grad_context.astype(BF16)
    context, grad_query, grad_memory = attention(lengths, queries, memory_heads, grad_context)
    def block_at(array, place):
        at = lax.rem(place + 2 * heads_axis, heads_axis) * block
        return lax.dynamic_slice_in_dim(array, at, block, array.ndim - 2)

    def first_block(parts):
        return block_at(parts, head_place - 1)

    def summed(got, parts, step):
        return got.astype(F32) + block_at(parts, head_place - 2 - step).astype(F32)

    def my_rows(array):
        return block_at(array, head_place)

    def place_rows(whole, rows, step, column=0):
        at = lax.rem(head_place - step + heads_axis, heads_axis) * block
        return lax.dynamic_update_slice(whole, rows, (at, column))

    def piled(parts):
        return jnp.stack([p.astype(BF16) for p in parts])

    last = heads_axis - 1
    def send_out(x):
        return head_shift(x, 1, DECODER)

    def send_memory(x):
        return head_shift(x, 1, ENCODER)

    def whole_rows(pieces):
        whole = jnp.zeros((block, width), F32)
        for k in range(chips):
            whole = lax.dynamic_update_slice_in_dim(whole, pieces[k], chip_at(-k) * span, 1)
        return whole

    back_parts = piled(dot_last(grad_query, w) for w in [first_chip] + first_far)
    back_held = first_block(back_parts)
    back_got = send_out(back_held)
    out_parts = piled(dot_last(context, w) for w in [second_chip] + second_far)
    out_held = first_block(out_parts)
    out_got = send_out(out_held)
    leaving = pass_on(grad_memory.reshape(2 * length, columns), back_held)
    leaving = leaving.reshape(2, length, columns)
    grad_memory, *far_memory = [home_shift(leaving, k) for k in range(chips)]

    memory_parts = piled(
        dot_last(g[0], first_chip) + dot_last(g[1], second_chip)
        for g in [grad_memory] + far_memory
    )
    memory_held = first_block(memory_parts)
    memory_got = send_memory(memory_held)

    def at(step):
        return lax.rem(head_place + 2 * heads_axis - step, heads_axis)

    for step in range(last):
        kind = BF16 if step < last - 1 else F32
        back_held = add_block(back_got, back_parts, at(2 + step), kind, out_held)
        if step == 0:
            moved = []
            for k in others:
                parts = [chip_columns(normed, k), chip_columns(grad_out, k), grad_query, context]
                moved.append(chip_shift(join(parts, back_held), k, DECODER))
        if step < last - 1:
            back_got = send_out(back_held)
            out_held = add_block(out_got, out_parts, at(2 + step), kind, back_held)
            out_got = send_out(out_held)
        memory_held = add_block(memory_got, memory_parts, at(2 + step), kind, back_held)
        if step < last - 1:
            memory_got = send_memory(memory_held)
    back_sum, memory_sum = back_held, memory_held

    homes = [chip_shift(memory_sum[k].astype(BF16), -k, ENCODER).astype(F32) for k in others]
    grad_normed = whole_rows(
        [jnp.where(encoder, memory_sum[0], back_sum[0])]
        + [jnp.where(encoder, homes[chips - 1 - k], back_sum[k]) for k in others]
    )
    grad_normed = grad_normed + jnp.where(encoder, my_rows(cotangent[0, 0]).astype(F32), 0.0)
    my_inverse = my_rows(inverse)
    my_unit = my_rows(states).astype(F32) * my_inverse
    residual = jnp.where(encoder, 0.0, my_rows(grad_out).astype(F32))
    scaled = grad_normed * gains
    inner = jnp.mean(scaled * my_unit, axis=-1, keepdims=True)
    grad_rows = (my_inverse * (scaled - my_unit * inner) + residual).astype(BF16)

    back_held = grad_rows
    back_got = head_shift(back_held, 1)
    gain_part = jnp.sum(grad_normed * my_unit, axis=0, keepdims=True)
    gain_parts = [head_shift(gain_part, k) for k in range(1, heads_axis)]
    out_sum = add_block(out_got, out_parts, at(1 + last), F32, back_held)
    out_held = (my_rows(states).astype(F32) + whole_rows(out_sum)).astype(BF16)
    out_got = send_out(out_held)
    arrivals = [(out_held, back_held)]

    decoder, always = ~encoder, jnp.bool_(True)

    def place_grad(whole, rows, step, *before):
        return place_block(whole, length, rows, at(step), None, always, *before)

    def place_out(whole, rows, step, *before):
        return place_block(whole, length, rows, at(step), normed, decoder, *before)

    def next_round(step, back_got, out_got, grad_states, result, token, first, then):
        arrived = back_got
        if step < last:
            back_got = head_shift(arrived, 1)
        grad_states, token = place_grad(grad_states, arrived, step, token, *first)
        arrived = out_got
        if step < last:
            out_got = send_out(arrived)
        result, token = place_out(result, arrived, step, token, *then)
        return back_got, out_got, grad_states, result, token

    arrived = back_got
    back_got = head_shift(arrived, 1)
    grad_states, token = place_grad(None, arrived, 1, out_held)
    arrived = out_got
    out_got = send_out(arrived)
    result, token = place_out(None, arrived, 1, token)
    grad_states, token = place_grad(grad_states, back_held, 0, token)
    result, token = place_out(result, out_held, 0, token)
    for part in gain_parts:
        gain_part = gain_part + part
    gain_part = pass_on(gain_part, back_got)
    gain_chip = chip_columns(gain_part, 0)
    gain_far = [chip_shift(chip_columns(gain_part, k), k) for k in others]
    left, right = [near_normed], [second_left]
    grads_first = [jnp.where(encoder, grad_memory[0], grad_query)]
    grads_second = [jnp.where(encoder, grad_memory[1], context)]
    for k in others:
        pieces = jnp.split(moved[k - 1], (span, 2 * span, 2 * span + columns), axis=1)
        left.append(jnp.where(encoder, far_normed[k - 1], pieces[0]))
        right.append(jnp.where(encoder, far_normed[k - 1], pieces[1]))
        grads_first.append(jnp.where(encoder, far_memory[k - 1][0], pieces[2]))
        grads_second.append(jnp.where(encoder, far_memory[k - 1][1], pieces[3]))

    def weight_grads(half):
        def one(rows, grads):
            rows, grads = jnp.concatenate(rows, axis=0), jnp.concatenate(grads, axis=0)
            return dot_rows(lax.dynamic_slice_in_dim(rows, half * tile, tile, 1), grads)

        return one(left, grads_first), one(right, grads_second)

    halves = jnp.stack([x.astype(BF16) for x in weight_grads(1 - core)])
    swapped = core_swap(halves)
    for step in range(2, last):
        back_got, out_got, grad_states, result, token = next_round(
            step, back_got, out_got, grad_states, result, token, [gain_part], [halves]
        )
    for part in gain_far:
        gain_chip = gain_chip + part
    gain_sum = lax.dynamic_slice_in_dim(gain_chip, core * tile, tile, 1)
    gain_sum = gain_sum + core_swap(
        lax.dynamic_slice_in_dim(gain_chip, (1 - core) * tile, tile, 1)
    )
    first_sum, second_sum = weight_grads(core)
    first_sum = first_sum + swapped[0].astype(F32)
    second_sum = second_sum + swapped[1].astype(F32)
    back_got, out_got, grad_states, result, token = next_round(
        last, back_got, out_got, grad_states, result, token, [gain_chip, first_sum], [second_sum]
    )
    return (
        result[None, None],
        grad_states[None, None],
        gain_sum,
        first_sum[None],
        second_sum[None],
    )


def solution(mesh):
    return jax.shard_map(
        shards,
        mesh=mesh,
        in_specs=(
            P("section", "dp", None, None),
            P("section", None),
            P("section", "dp", "mp"),
            P("section", "dp", "mp"),
            P("dp", None),
            P("section", "dp", None, None),
        ),
        out_specs=(
            P("section", "dp", None, None),
            P("section", "dp", None, None),
            P("section", "dp"),
            P("section", "dp", "mp"),
            P("section", "dp", "mp"),
        ),
        check_vma=False,
    )
```

```python
import functools
import math

import jax
import jax.numpy as jnp
from jax import lax
from jax.experimental import pallas as pl
from jax.experimental.pallas import tpu as pltpu
from jax.sharding import PartitionSpec as P

HEAD = 128
EPS = 1e-06
MASKED = -1e30
WAIT = 12 * 10**9
CORES = 2
F32 = jnp.float32
BF16 = jnp.bfloat16


def dot_rows(left, right):
    return lax.dot_general(left, right, (((0,), (0,)), ((), ())), preferred_element_type=F32)


def dot_last(left, right):
    return lax.dot_general(left, right, (((1,), (1,)), ((), ())), preferred_element_type=F32)


def dot_plain(left, right):
    return jnp.dot(left, right, preferred_element_type=F32)


BOTH, ENCODER, DECODER = (0, 1), (0,), (1,)


def permute(x, axis, to, sections):
    n = lax.axis_size(axis)
    if sections == BOTH:
        return lax.ppermute(x, axis, [(i, to(i, n)) for i in range(n)])
    pairs = [(s * n + i, s * n + to(i, n)) for s in sections for i in range(n)]
    return lax.ppermute(x, ("section", axis), pairs)


def core_swap(x, sections=BOTH):
    return permute(x, "dp", lambda i, n: i ^ 1, sections)


def chip_shift(x, by, sections=BOTH):
    return permute(x, "dp", lambda i, n: (i + by * CORES) % n, sections)


def home_shift(x, by):
    n = lax.axis_size("dp")
    pairs = [(n + i, (i + by * CORES) % n) for i in range(n)]
    return lax.ppermute(x, ("section", "dp"), pairs)


def head_shift(x, by, sections=BOTH):
    return permute(x, "mp", lambda i, n: (i + by) % n, sections)


ANYWHERE = pl.BlockSpec(memory_space=pl.ANY)


def add_kernel(place_ref, got_ref, part_ref, *refs):
    refs[-1][...] = (got_ref[...].astype(F32) + part_ref[...].astype(F32)).astype(refs[-1].dtype)


def add_block(got, parts, place, dtype, *before):
    seqs, tokens, features = got.shape
    steps = 2 if features % 256 == 0 else 1
    piece = features // steps
    block = pl.BlockSpec((seqs, tokens, piece), lambda i, at: (0, 0, i))
    return pl.pallas_call(
        add_kernel,
        grid_spec=pltpu.PrefetchScalarGridSpec(
            num_scalar_prefetch=1,
            grid=(steps,),
            in_specs=[
                block,
                pl.BlockSpec((seqs, tokens, piece), lambda i, at: (0, at[0], i)),
            ]
            + [ANYWHERE] * len(before),
            out_specs=block,
        ),
        out_shape=jax.ShapeDtypeStruct(got.shape, dtype),
        compiler_params=pltpu.CompilerParams(vmem_limit_bytes=32 * 2**20),
        cost_estimate=pl.CostEstimate(flops=WAIT, bytes_accessed=0, transcendentals=0),
        name="add_block",
    )(place.reshape(1), got, parts, *before)


def place_kernel(place_ref, rows_ref, other_ref, *refs):
    out_ref, token_ref, ready, sem = refs[-4:]
    token_ref[...] = jnp.zeros_like(token_ref)
    tokens = rows_ref.shape[0]
    at = pl.multiple_of(place_ref[0] * tokens, tokens)
    ready[...] = jnp.where(place_ref[1] == 1, rows_ref[...], other_ref[...])
    copy = pltpu.make_async_copy(ready, out_ref.at[pl.ds(at, tokens)], sem)
    copy.start()
    copy.wait()


def place_block(whole, length, rows, place, other, wanted, *before):
    tokens, features = rows.shape
    where = jnp.stack([place, wanted.astype(jnp.int32)])
    mine = pl.BlockSpec((tokens, features), lambda i, at: (0, 0))
    whole = [] if whole is None else [whole]
    if other is None:
        other, other_block = rows, mine
    else:
        other_block = pl.BlockSpec((tokens, features), lambda i, at: (at[0], 0))
    return pl.pallas_call(
        place_kernel,
        grid_spec=pltpu.PrefetchScalarGridSpec(
            num_scalar_prefetch=1,
            grid=(1,),
            in_specs=[mine, other_block] + [ANYWHERE] * len(whole + list(before)),
            out_specs=[ANYWHERE, pl.BlockSpec((8, 128), lambda i, at: (0, 0))],
            scratch_shapes=[
                pltpu.VMEM((tokens, features), rows.dtype),
                pltpu.SemaphoreType.DMA,
            ],
        ),
        out_shape=[
            jax.ShapeDtypeStruct((length, features), rows.dtype),
            jax.ShapeDtypeStruct((8, 128), F32),
        ],
        input_output_aliases={3: 0} if whole else {},
        compiler_params=pltpu.CompilerParams(vmem_limit_bytes=32 * 2**20),
        cost_estimate=pl.CostEstimate(flops=WAIT, bytes_accessed=0, transcendentals=0),
        name="place_block",
    )(where, rows, other, *whole, *before)


def pass_kernel(rows_ref, *refs):
    refs[-1][...] = rows_ref[...]


def pass_on(rows, *before):
    block = pl.BlockSpec(rows.shape, lambda i: (0, 0))
    return pl.pallas_call(
        pass_kernel,
        grid=(1,),
        in_specs=[block] + [ANYWHERE] * len(before),
        out_specs=block,
        out_shape=jax.ShapeDtypeStruct(rows.shape, rows.dtype),
        compiler_params=pltpu.CompilerParams(vmem_limit_bytes=32 * 2**20),
        cost_estimate=pl.CostEstimate(flops=10**9, bytes_accessed=0, transcendentals=0),
        name="pass_on",
    )(rows, *before)


def join_kernel(count, *refs):
    at = 0
    for ref in refs[:count]:
        refs[-1][:, at : at + ref.shape[1]] = ref[...]
        at += ref.shape[1]


def join(parts, *before):
    rows = parts[0].shape[0]
    steps = 2 if rows % 32 == 0 else 1
    width = sum(p.shape[1] for p in parts)

    def block(columns):
        return pl.BlockSpec((rows // steps, columns), lambda i: (i, 0))

    return pl.pallas_call(
        functools.partial(join_kernel, len(parts)),
        grid=(steps,),
        in_specs=[block(p.shape[1]) for p in parts] + [ANYWHERE] * len(before),
        out_specs=block(width),
        out_shape=jax.ShapeDtypeStruct((rows, width), parts[0].dtype),
        compiler_params=pltpu.CompilerParams(vmem_limit_bytes=32 * 2**20),
        cost_estimate=pl.CostEstimate(flops=10**9, bytes_accessed=0, transcendentals=0),
        name="join",
    )(*parts, *before)


def attention_kernel(lengths_ref, q_ref, kv_ref, g_ref, ctx_ref, gq_ref, gkv_ref):
    scale = 1.0 / math.sqrt(HEAD)
    q, k, v, g = q_ref[...], kv_ref[0], kv_ref[1], g_ref[...]
    scores = dot_last(q, k) * scale
    column = lax.broadcasted_iota(jnp.int32, scores.shape, 1)
    scores = jnp.where(column < lengths_ref[0, 0], scores, MASKED)
    top = jnp.max(scores, axis=-1, keepdims=True)
    raised = jnp.exp(scores - top)
    weights = raised / jnp.sum(raised, axis=-1, keepdims=True)
    low = weights.astype(BF16)
    ctx_ref[...] = dot_plain(low, v).astype(BF16)
    gkv_ref[1] = dot_rows(low, g).astype(BF16)
    grad_weights = dot_last(g, v)
    centered = grad_weights - jnp.sum(weights * grad_weights, axis=-1, keepdims=True)
    grad_scores = (weights * centered * scale).astype(BF16)
    gq_ref[...] = dot_plain(grad_scores, k).astype(BF16)
    gkv_ref[0] = dot_rows(grad_scores, q).astype(BF16)


def attention(lengths, q, kv, g):
    rows, columns = q.shape
    block = pl.BlockSpec((rows, HEAD), lambda h: (0, h))
    pair = pl.BlockSpec((2, rows, HEAD), lambda h: (0, 0, h))
    shape = jax.ShapeDtypeStruct((rows, columns), BF16)
    heads = columns // HEAD
    return pl.pallas_call(
        attention_kernel,
        grid=(heads,),
        in_specs=[pl.BlockSpec(memory_space=pltpu.SMEM), block, pair, block],
        out_specs=[block, block, pair],
        out_shape=[shape, shape, jax.ShapeDtypeStruct((2, rows, columns), BF16)],
        compiler_params=pltpu.CompilerParams(vmem_limit_bytes=32 * 2**20),
        cost_estimate=pl.CostEstimate(
            flops=14 * rows * rows * columns,
            bytes_accessed=16 * rows * columns,
            transcendentals=heads * rows * rows,
        ),
        name="attention",
    )(lengths, q, kv, g)


def shards(hidden, gain, w_first, w_second, lengths, cotangent):
    encoder = lax.axis_index("section") == 0
    place = lax.axis_index("dp")
    chip, core = place // CORES, lax.rem(place, CORES)
    head_place = lax.axis_index("mp")
    heads_axis = lax.axis_size("mp")
    chips = lax.axis_size("dp") // CORES
    states = hidden[0, 0]
    length, width = states.shape
    gains = gain[0][None, :]
    tile = w_first.shape[1]
    span = CORES * tile
    columns = w_first.shape[2]
    block = length // heads_axis
    others = range(1, chips)

    def chip_at(k):
        return lax.rem(chip + k + chips, chips)

    def chip_columns(array, k):
        return lax.dynamic_slice_in_dim(array, chip_at(k) * span, span, 1)

    def in_order(own, other):
        ahead = [jnp.where(core == 0, a, b) for a, b in zip(own, other)]
        behind = [jnp.where(core == 0, b, a) for a, b in zip(own, other)]
        return jnp.concatenate(ahead + behind, axis=0)

    def whole_chip(own):
        return in_order([own], [core_swap(own)])

    first, second = w_first[0], w_second[0]
    first_far = [chip_shift(first, k, DECODER) for k in others]
    far_states = [chip_shift(chip_columns(states, k), k, ENCODER) for k in others]
    first_chip = whole_chip(first)
    second_chip = whole_chip(second)
    wide = states.astype(F32)
    inverse = lax.rsqrt(jnp.mean(wide * wide, axis=-1, keepdims=True) + EPS)
    inverse_row = inverse.reshape(1, length)
    far_inverse = [chip_shift(inverse_row, k, ENCODER).reshape(length, 1) for k in others]
    unit = wide * inverse
    normed = (unit * gains).astype(BF16)
    keep = jnp.arange(length)[:, None] < lengths[0, 1]
    grad_out = jnp.where(keep, cotangent[0, 0], jnp.zeros((), BF16))

    near_normed = chip_columns(normed, 0)
    second_left = jnp.where(encoder, near_normed, chip_columns(grad_out, 0))
    own_first = dot_plain(near_normed, first_chip)
    own_second = dot_plain(second_left, second_chip)
    normed_columns = [chip_columns(normed, -k) for k in others]
    grad_columns = [chip_columns(grad_out, -k) for k in others]
    far_states, own_first, own_second, normed_columns, grad_columns = lax.optimization_barrier(
        (far_states, own_first, own_second, normed_columns, grad_columns)
    )
    gains_chip = chip_columns(gains, 0)
    far_normed = [
        (rows.astype(F32) * inv * gains_chip).astype(BF16)
        for rows, inv in zip(far_states, far_inverse)
    ]

    both = jnp.stack([own_first, own_second])
    for k in others:
        part = jnp.stack(
            [dot_plain(far_normed[k - 1], w).astype(BF16) for w in (first_chip, second_chip)]
        )
        both = both + chip_shift(part, -k, ENCODER).astype(F32)
    both, first_far = lax.optimization_barrier((both.astype(BF16), first_far))
    second_far = [chip_shift(second, k, DECODER) for k in others]
    memory_heads = lax.ppermute(both, "section", [(0, 1)])

    first_far = [whole_chip(w) for w in first_far]
    queries, grad_context = own_first, own_second
    for k in others:
        queries = queries + dot_plain(normed_columns[k - 1], first_far[k - 1])
    queries = queries.astype(BF16)
    memory_heads, second_far, queries = lax.optimization_barrier(
        (memory_heads, second_far, queries)
    )
    second_far = [whole_chip(w) for w in second_far]
    for k in others:
        grad_context = grad_context + dot_plain(grad_columns[k - 1], second_far[k - 1])
    grad_context = grad_context.astype(BF16)
    context, grad_query, grad_memory = attention(lengths, queries, memory_heads, grad_context)
    def block_at(array, place):
        at = lax.rem(place + 2 * heads_axis, heads_axis) * block
        return lax.dynamic_slice_in_dim(array, at, block, array.ndim - 2)

    def first_block(parts):
        return block_at(parts, head_place - 1)

    def summed(got, parts, step):
        return got.astype(F32) + block_at(parts, head_place - 2 - step).astype(F32)

    def my_rows(array):
        return block_at(array, head_place)

    def place_rows(whole, rows, step, column=0):
        at = lax.rem(head_place - step + heads_axis, heads_axis) * block
        return lax.dynamic_update_slice(whole, rows, (at, column))

    def piled(parts):
        return jnp.stack([p.astype(BF16) for p in parts])

    last = heads_axis - 1
    def send_out(x):
        return head_shift(x, 1, DECODER)

    def send_memory(x):
        return head_shift(x, 1, ENCODER)

    def whole_rows(pieces):
        whole = jnp.zeros((block, width), F32)
        for k in range(chips):
            whole = lax.dynamic_update_slice_in_dim(whole, pieces[k], chip_at(-k) * span, 1)
        return whole

    back_parts = piled(dot_last(grad_query, w) for w in [first_chip] + first_far)
    back_held = first_block(back_parts)
    back_got = send_out(back_held)
    out_parts = piled(dot_last(context, w) for w in [second_chip] + second_far)
    out_held = first_block(out_parts)
    out_got = send_out(out_held)
    leaving = pass_on(grad_memory.reshape(2 * length, columns), back_held)
    leaving = leaving.reshape(2, length, columns)
    grad_memory, *far_memory = [home_shift(leaving, k) for k in range(chips)]

    memory_parts = piled(
        dot_last(g[0], first_chip) + dot_last(g[1], second_chip)
        for g in [grad_memory] + far_memory
    )
    memory_held = first_block(memory_parts)
    memory_got = send_memory(memory_held)

    def at(step):
        return lax.rem(head_place + 2 * heads_axis - step, heads_axis)

    for step in range(last):
        kind = BF16 if step < last - 1 else F32
        back_held = add_block(back_got, back_parts, at(2 + step), kind, out_held)
        if step == 0:
            moved = []
            for k in others:
                parts = [chip_columns(normed, k), chip_columns(grad_out, k), grad_query, context]
                moved.append(chip_shift(join(parts, back_held), k, DECODER))
        if step < last - 1:
            back_got = send_out(back_held)
            out_held = add_block(out_got, out_parts, at(2 + step), kind, back_held)
            out_got = send_out(out_held)
        memory_held = add_block(memory_got, memory_parts, at(2 + step), kind, back_held)
        if step < last - 1:
            memory_got = send_memory(memory_held)
    back_sum, memory_sum = back_held, memory_held

    homes = [chip_shift(memory_sum[k].astype(BF16), -k, ENCODER).astype(F32) for k in others]
    grad_normed = whole_rows(
        [jnp.where(encoder, memory_sum[0], back_sum[0])]
        + [jnp.where(encoder, homes[chips - 1 - k], back_sum[k]) for k in others]
    )
    grad_normed = grad_normed + jnp.where(encoder, my_rows(cotangent[0, 0]).astype(F32), 0.0)
    my_inverse = my_rows(inverse)
    my_unit = my_rows(states).astype(F32) * my_inverse
    residual = jnp.where(encoder, 0.0, my_rows(grad_out).astype(F32))
    scaled = grad_normed * gains
    inner = jnp.mean(scaled * my_unit, axis=-1, keepdims=True)
    grad_rows = (my_inverse * (scaled - my_unit * inner) + residual).astype(BF16)

    back_held = grad_rows
    back_got = head_shift(back_held, 1)
    gain_part = jnp.sum(grad_normed * my_unit, axis=0, keepdims=True)
    gain_parts = [head_shift(gain_part, k) for k in range(1, heads_axis)]
    out_sum = add_block(out_got, out_parts, at(1 + last), F32, back_held)
    out_held = (my_rows(states).astype(F32) + whole_rows(out_sum)).astype(BF16)
    out_got = send_out(out_held)
    arrivals = [(out_held, back_held)]

    own_out_rows = out_held
    decoder, always = ~encoder, jnp.bool_(True)

    def place_grad(whole, rows, step, *before):
        return place_block(whole, length, rows, at(step), None, always, *before)

    def place_out(whole, rows, step, *before):
        return place_block(whole, length, rows, at(step), normed, decoder, *before)

    def next_round(step, back_got, out_got, grad_states, result, token, first, then):
        arrived = back_got
        if step < last:
            back_got = head_shift(arrived, 1)
        grad_states, token = place_grad(grad_states, arrived, step, token, *first)
        arrived = out_got
        if step < last:
            out_got = send_out(arrived)
        result, token = place_out(result, arrived, step, token, *then)
        return back_got, out_got, grad_states, result, token

    arrived = back_got
    back_got = head_shift(arrived, 1)
    grad_states, token = place_grad(None, arrived, 1, out_held)
    arrived = out_got
    out_got = send_out(arrived)
    result, token = place_out(None, arrived, 1, token)
    for part in gain_parts:
        gain_part = gain_part + part
    gain_part = pass_on(gain_part, back_got)
    gain_chip = chip_columns(gain_part, 0)
    gain_far = [chip_shift(chip_columns(gain_part, k), k) for k in others]
    left, right = [near_normed], [second_left]
    grads_first = [jnp.where(encoder, grad_memory[0], grad_query)]
    grads_second = [jnp.where(encoder, grad_memory[1], context)]
    for k in others:
        pieces = jnp.split(moved[k - 1], (span, 2 * span, 2 * span + columns), axis=1)
        left.append(jnp.where(encoder, far_normed[k - 1], pieces[0]))
        right.append(jnp.where(encoder, far_normed[k - 1], pieces[1]))
        grads_first.append(jnp.where(encoder, far_memory[k - 1][0], pieces[2]))
        grads_second.append(jnp.where(encoder, far_memory[k - 1][1], pieces[3]))

    def weight_grads(half):
        def one(rows, grads):
            rows, grads = jnp.concatenate(rows, axis=0), jnp.concatenate(grads, axis=0)
            return dot_rows(lax.dynamic_slice_in_dim(rows, half * tile, tile, 1), grads)

        return one(left, grads_first), one(right, grads_second)

    halves = jnp.stack([x.astype(BF16) for x in weight_grads(1 - core)])
    swapped = core_swap(halves)
    for step in range(2, last):
        back_got, out_got, grad_states, result, token = next_round(
            step, back_got, out_got, grad_states, result, token, [gain_part], [halves]
        )
    for part in gain_far:
        gain_chip = gain_chip + part
    gain_sum = lax.dynamic_slice_in_dim(gain_chip, core * tile, tile, 1)
    gain_sum = gain_sum + core_swap(
        lax.dynamic_slice_in_dim(gain_chip, (1 - core) * tile, tile, 1)
    )
    first_sum, second_sum = weight_grads(core)
    first_sum = first_sum + swapped[0].astype(F32)
    second_sum = second_sum + swapped[1].astype(F32)
    grad_states, token = place_grad(grad_states, grad_rows, 0, token)
    result, token = place_out(result, own_out_rows, 0, token)
    back_got, out_got, grad_states, result, token = next_round(
        last, back_got, out_got, grad_states, result, token, [gain_chip, first_sum], [second_sum]
    )
    return (
        result[None, None],
        grad_states[None, None],
        gain_sum,
        first_sum[None],
        second_sum[None],
    )


def solution(mesh):
    return jax.shard_map(
        shards,
        mesh=mesh,
        in_specs=(
            P("section", "dp", None, None),
            P("section", None),
            P("section", "dp", "mp"),
            P("section", "dp", "mp"),
            P("dp", None),
            P("section", "dp", None, None),
        ),
        out_specs=(
            P("section", "dp", None, None),
            P("section", "dp", None, None),
            P("section", "dp"),
            P("section", "dp", "mp"),
            P("section", "dp", "mp"),
        ),
        check_vma=False,
    )
```

```python
import functools
import math

import jax
import jax.numpy as jnp
from jax import lax
from jax.experimental import pallas as pl
from jax.experimental.pallas import tpu as pltpu
from jax.sharding import PartitionSpec as P

HEAD = 128
EPS = 1e-06
MASKED = -1e30
WAIT = 12 * 10**9
CORES = 2
F32 = jnp.float32
BF16 = jnp.bfloat16


def dot_rows(left, right):
    return lax.dot_general(left, right, (((0,), (0,)), ((), ())), preferred_element_type=F32)


def dot_last(left, right):
    return lax.dot_general(left, right, (((1,), (1,)), ((), ())), preferred_element_type=F32)


def dot_plain(left, right):
    return jnp.dot(left, right, preferred_element_type=F32)


BOTH, ENCODER, DECODER = (0, 1), (0,), (1,)


def permute(x, axis, to, sections):
    n = lax.axis_size(axis)
    if sections == BOTH:
        return lax.ppermute(x, axis, [(i, to(i, n)) for i in range(n)])
    pairs = [(s * n + i, s * n + to(i, n)) for s in sections for i in range(n)]
    return lax.ppermute(x, ("section", axis), pairs)


def core_swap(x, sections=BOTH):
    return permute(x, "dp", lambda i, n: i ^ 1, sections)


def chip_shift(x, by, sections=BOTH):
    return permute(x, "dp", lambda i, n: (i + by * CORES) % n, sections)


def home_shift(x, by):
    n = lax.axis_size("dp")
    pairs = [(n + i, (i + by * CORES) % n) for i in range(n)]
    return lax.ppermute(x, ("section", "dp"), pairs)


def head_shift(x, by, sections=BOTH):
    return permute(x, "mp", lambda i, n: (i + by) % n, sections)


ANYWHERE = pl.BlockSpec(memory_space=pl.ANY)


def add_kernel(place_ref, got_ref, part_ref, *refs):
    refs[-1][...] = (got_ref[...].astype(F32) + part_ref[...].astype(F32)).astype(refs[-1].dtype)


def add_block(got, parts, place, dtype, *before):
    seqs, tokens, features = got.shape
    steps = 2 if features % 256 == 0 else 1
    piece = features // steps
    block = pl.BlockSpec((seqs, tokens, piece), lambda i, at: (0, 0, i))
    return pl.pallas_call(
        add_kernel,
        grid_spec=pltpu.PrefetchScalarGridSpec(
            num_scalar_prefetch=1,
            grid=(steps,),
            in_specs=[
                block,
                pl.BlockSpec((seqs, tokens, piece), lambda i, at: (0, at[0], i)),
            ]
            + [ANYWHERE] * len(before),
            out_specs=block,
        ),
        out_shape=jax.ShapeDtypeStruct(got.shape, dtype),
        compiler_params=pltpu.CompilerParams(vmem_limit_bytes=32 * 2**20),
        cost_estimate=pl.CostEstimate(flops=WAIT, bytes_accessed=0, transcendentals=0),
        name="add_block",
    )(place.reshape(1), got, parts, *before)


def place_kernel(place_ref, rows_ref, other_ref, *refs):
    out_ref, token_ref, ready, sem = refs[-4:]
    token_ref[...] = jnp.zeros_like(token_ref)
    tokens = rows_ref.shape[0]
    at = pl.multiple_of(place_ref[0] * tokens, tokens)
    ready[...] = jnp.where(place_ref[1] == 1, rows_ref[...], other_ref[...])
    copy = pltpu.make_async_copy(ready, out_ref.at[pl.ds(at, tokens)], sem)
    copy.start()
    copy.wait()


def place_block(whole, length, rows, place, other, wanted, *before):
    tokens, features = rows.shape
    where = jnp.stack([place, wanted.astype(jnp.int32)])
    mine = pl.BlockSpec((tokens, features), lambda i, at: (0, 0))
    whole = [] if whole is None else [whole]
    if other is None:
        other, other_block = rows, mine
    else:
        other_block = pl.BlockSpec((tokens, features), lambda i, at: (at[0], 0))
    return pl.pallas_call(
        place_kernel,
        grid_spec=pltpu.PrefetchScalarGridSpec(
            num_scalar_prefetch=1,
            grid=(1,),
            in_specs=[mine, other_block] + [ANYWHERE] * len(whole + list(before)),
            out_specs=[ANYWHERE, pl.BlockSpec((8, 128), lambda i, at: (0, 0))],
            scratch_shapes=[
                pltpu.VMEM((tokens, features), rows.dtype),
                pltpu.SemaphoreType.DMA,
            ],
        ),
        out_shape=[
            jax.ShapeDtypeStruct((length, features), rows.dtype),
            jax.ShapeDtypeStruct((8, 128), F32),
        ],
        input_output_aliases={3: 0} if whole else {},
        compiler_params=pltpu.CompilerParams(vmem_limit_bytes=32 * 2**20),
        cost_estimate=pl.CostEstimate(flops=WAIT, bytes_accessed=0, transcendentals=0),
        name="place_block",
    )(where, rows, other, *whole, *before)


def pass_kernel(rows_ref, *refs):
    refs[-1][...] = rows_ref[...]


def pass_on(rows, *before):
    block = pl.BlockSpec(rows.shape, lambda i: (0, 0))
    return pl.pallas_call(
        pass_kernel,
        grid=(1,),
        in_specs=[block] + [ANYWHERE] * len(before),
        out_specs=block,
        out_shape=jax.ShapeDtypeStruct(rows.shape, rows.dtype),
        compiler_params=pltpu.CompilerParams(vmem_limit_bytes=32 * 2**20),
        cost_estimate=pl.CostEstimate(flops=10**9, bytes_accessed=0, transcendentals=0),
        name="pass_on",
    )(rows, *before)


def join_kernel(count, *refs):
    at = 0
    for ref in refs[:count]:
        refs[-1][:, at : at + ref.shape[1]] = ref[...]
        at += ref.shape[1]


def join(parts, *before):
    rows = parts[0].shape[0]
    steps = 2 if rows % 32 == 0 else 1
    width = sum(p.shape[1] for p in parts)

    def block(columns):
        return pl.BlockSpec((rows // steps, columns), lambda i: (i, 0))

    return pl.pallas_call(
        functools.partial(join_kernel, len(parts)),
        grid=(steps,),
        in_specs=[block(p.shape[1]) for p in parts] + [ANYWHERE] * len(before),
        out_specs=block(width),
        out_shape=jax.ShapeDtypeStruct((rows, width), parts[0].dtype),
        compiler_params=pltpu.CompilerParams(vmem_limit_bytes=32 * 2**20),
        cost_estimate=pl.CostEstimate(flops=10**9, bytes_accessed=0, transcendentals=0),
        name="join",
    )(*parts, *before)


def attention_kernel(lengths_ref, q_ref, kv_ref, g_ref, ctx_ref, gq_ref, gkv_ref):
    scale = 1.0 / math.sqrt(HEAD)
    q, k, v, g = q_ref[...], kv_ref[0], kv_ref[1], g_ref[...]
    scores = dot_last(q, k) * scale
    column = lax.broadcasted_iota(jnp.int32, scores.shape, 1)
    scores = jnp.where(column < lengths_ref[0, 0], scores, MASKED)
    top = jnp.max(scores, axis=-1, keepdims=True)
    raised = jnp.exp(scores - top)
    weights = raised / jnp.sum(raised, axis=-1, keepdims=True)
    low = weights.astype(BF16)
    ctx_ref[...] = dot_plain(low, v).astype(BF16)
    gkv_ref[1] = dot_rows(low, g).astype(BF16)
    grad_weights = dot_last(g, v)
    centered = grad_weights - jnp.sum(weights * grad_weights, axis=-1, keepdims=True)
    grad_scores = (weights * centered * scale).astype(BF16)
    gq_ref[...] = dot_plain(grad_scores, k).astype(BF16)
    gkv_ref[0] = dot_rows(grad_scores, q).astype(BF16)


def attention(lengths, q, kv, g):
    rows, columns = q.shape
    block = pl.BlockSpec((rows, HEAD), lambda h: (0, h))
    pair = pl.BlockSpec((2, rows, HEAD), lambda h: (0, 0, h))
    shape = jax.ShapeDtypeStruct((rows, columns), BF16)
    heads = columns // HEAD
    return pl.pallas_call(
        attention_kernel,
        grid=(heads,),
        in_specs=[pl.BlockSpec(memory_space=pltpu.SMEM), block, pair, block],
        out_specs=[block, block, pair],
        out_shape=[shape, shape, jax.ShapeDtypeStruct((2, rows, columns), BF16)],
        compiler_params=pltpu.CompilerParams(vmem_limit_bytes=32 * 2**20),
        cost_estimate=pl.CostEstimate(
            flops=14 * rows * rows * columns,
            bytes_accessed=16 * rows * columns,
            transcendentals=heads * rows * rows,
        ),
        name="attention",
    )(lengths, q, kv, g)


def shards(hidden, gain, w_first, w_second, lengths, cotangent):
    encoder = lax.axis_index("section") == 0
    place = lax.axis_index("dp")
    chip, core = place // CORES, lax.rem(place, CORES)
    head_place = lax.axis_index("mp")
    heads_axis = lax.axis_size("mp")
    chips = lax.axis_size("dp") // CORES
    states = hidden[0, 0]
    length, width = states.shape
    gains = gain[0][None, :]
    tile = w_first.shape[1]
    span = CORES * tile
    columns = w_first.shape[2]
    block = length // heads_axis
    others = range(1, chips)

    def chip_at(k):
        return lax.rem(chip + k + chips, chips)

    def chip_columns(array, k):
        return lax.dynamic_slice_in_dim(array, chip_at(k) * span, span, 1)

    def in_order(own, other):
        ahead = [jnp.where(core == 0, a, b) for a, b in zip(own, other)]
        behind = [jnp.where(core == 0, b, a) for a, b in zip(own, other)]
        return jnp.concatenate(ahead + behind, axis=0)

    def whole_chip(own):
        return in_order([own], [core_swap(own)])

    first, second = w_first[0], w_second[0]
    first_far = [chip_shift(first, k, DECODER) for k in others]
    far_states = [chip_shift(chip_columns(states, k), k, ENCODER) for k in others]
    first_chip = whole_chip(first)
    second_chip = whole_chip(second)
    wide = states.astype(F32)
    inverse = lax.rsqrt(jnp.mean(wide * wide, axis=-1, keepdims=True) + EPS)
    inverse_row = inverse.reshape(1, length)
    far_inverse = [chip_shift(inverse_row, k, ENCODER).reshape(length, 1) for k in others]
    unit = wide * inverse
    normed = (unit * gains).astype(BF16)
    keep = jnp.arange(length)[:, None] < lengths[0, 1]
    grad_out = jnp.where(keep, cotangent[0, 0], jnp.zeros((), BF16))

    near_normed = chip_columns(normed, 0)
    second_left = jnp.where(encoder, near_normed, chip_columns(grad_out, 0))
    own_first = dot_plain(near_normed, first_chip)
    own_second = dot_plain(second_left, second_chip)
    normed_columns = [chip_columns(normed, -k) for k in others]
    grad_columns = [chip_columns(grad_out, -k) for k in others]
    far_states, own_first, own_second, normed_columns, grad_columns = lax.optimization_barrier(
        (far_states, own_first, own_second, normed_columns, grad_columns)
    )
    gains_chip = chip_columns(gains, 0)
    far_normed = [
        (rows.astype(F32) * inv * gains_chip).astype(BF16)
        for rows, inv in zip(far_states, far_inverse)
    ]

    both = jnp.stack([own_first, own_second])
    for k in others:
        part = jnp.stack(
            [dot_plain(far_normed[k - 1], w).astype(BF16) for w in (first_chip, second_chip)]
        )
        both = both + chip_shift(part, -k, ENCODER).astype(F32)
    both, first_far = lax.optimization_barrier((both.astype(BF16), first_far))
    second_far = [chip_shift(second, k, DECODER) for k in others]
    memory_heads = lax.ppermute(both, "section", [(0, 1)])

    first_far = [whole_chip(w) for w in first_far]
    queries, grad_context = own_first, own_second
    for k in others:
        queries = queries + dot_plain(normed_columns[k - 1], first_far[k - 1])
    queries = queries.astype(BF16)
    memory_heads, second_far, queries = lax.optimization_barrier(
        (memory_heads, second_far, queries)
    )
    second_far = [whole_chip(w) for w in second_far]
    for k in others:
        grad_context = grad_context + dot_plain(grad_columns[k - 1], second_far[k - 1])
    grad_context = grad_context.astype(BF16)
    context, grad_query, grad_memory = attention(lengths, queries, memory_heads, grad_context)
    def block_at(array, place):
        at = lax.rem(place + 2 * heads_axis, heads_axis) * block
        return lax.dynamic_slice_in_dim(array, at, block, array.ndim - 2)

    def first_block(parts):
        return block_at(parts, head_place - 1)

    def summed(got, parts, step):
        return got.astype(F32) + block_at(parts, head_place - 2 - step).astype(F32)

    def my_rows(array):
        return block_at(array, head_place)

    def place_rows(whole, rows, step, column=0):
        at = lax.rem(head_place - step + heads_axis, heads_axis) * block
        return lax.dynamic_update_slice(whole, rows, (at, column))

    def piled(parts):
        return jnp.stack([p.astype(BF16) for p in parts])

    last = heads_axis - 1
    def send_out(x):
        return head_shift(x, 1, DECODER)

    def send_memory(x):
        return head_shift(x, 1, ENCODER)

    def whole_rows(pieces):
        whole = jnp.zeros((block, width), F32)
        for k in range(chips):
            whole = lax.dynamic_update_slice_in_dim(whole, pieces[k], chip_at(-k) * span, 1)
        return whole

    back_parts = piled(dot_last(grad_query, w) for w in [first_chip] + first_far)
    back_held = first_block(back_parts)
    back_got = send_out(back_held)
    out_parts = piled(dot_last(context, w) for w in [second_chip] + second_far)
    out_held = first_block(out_parts)
    out_got = send_out(out_held)
    leaving = pass_on(grad_memory.reshape(2 * length, columns), back_held)
    leaving = leaving.reshape(2, length, columns)
    grad_memory, *far_memory = [home_shift(leaving, k) for k in range(chips)]

    memory_parts = piled(
        dot_last(g[0], first_chip) + dot_last(g[1], second_chip)
        for g in [grad_memory] + far_memory
    )
    memory_held = first_block(memory_parts)
    memory_got = send_memory(memory_held)

    def at(step):
        return lax.rem(head_place + 2 * heads_axis - step, heads_axis)

    for step in range(last):
        kind = BF16 if step < last - 1 else F32
        back_held = add_block(back_got, back_parts, at(2 + step), kind, out_held)
        if step == 0:
            moved = []
            for k in others:
                parts = [chip_columns(normed, k), chip_columns(grad_out, k), grad_query, context]
                moved.append(chip_shift(join(parts, back_held), k, DECODER))
        if step < last - 1:
            back_got = send_out(back_held)
            out_held = add_block(out_got, out_parts, at(2 + step), kind, back_held)
            out_got = send_out(out_held)
        memory_held = add_block(memory_got, memory_parts, at(2 + step), kind, back_held)
        if step < last - 1:
            memory_got = send_memory(memory_held)
    back_sum, memory_sum = back_held, memory_held

    homes = [chip_shift(memory_sum[k].astype(BF16), -k, ENCODER).astype(F32) for k in others]
    grad_normed = whole_rows(
        [jnp.where(encoder, memory_sum[0], back_sum[0])]
        + [jnp.where(encoder, homes[chips - 1 - k], back_sum[k]) for k in others]
    )
    grad_normed = grad_normed + jnp.where(encoder, my_rows(cotangent[0, 0]).astype(F32), 0.0)
    my_inverse = my_rows(inverse)
    my_unit = my_rows(states).astype(F32) * my_inverse
    residual = jnp.where(encoder, 0.0, my_rows(grad_out).astype(F32))
    scaled = grad_normed * gains
    inner = jnp.mean(scaled * my_unit, axis=-1, keepdims=True)
    grad_rows = (my_inverse * (scaled - my_unit * inner) + residual).astype(BF16)

    back_held = grad_rows
    back_got = head_shift(back_held, 1)
    gain_part = jnp.sum(grad_normed * my_unit, axis=0, keepdims=True)
    gain_parts = [head_shift(gain_part, k) for k in range(1, heads_axis)]
    out_sum = add_block(out_got, out_parts, at(1 + last), F32, back_held)
    out_held = (my_rows(states).astype(F32) + whole_rows(out_sum)).astype(BF16)
    out_got = send_out(out_held)
    arrivals = [(out_held, back_held)]

    decoder, always = ~encoder, jnp.bool_(True)

    def place_grad(whole, rows, step, *before):
        return place_block(whole, length, rows, at(step), None, always, *before)

    def place_out(whole, rows, step, *before):
        return place_block(whole, length, rows, at(step), normed, decoder, *before)

    def next_round(step, back_got, out_got, grad_states, result, token, first, then):
        arrived = back_got
        if step < last:
            back_got = head_shift(arrived, 1)
        grad_states, token = place_grad(grad_states, arrived, step, token, *first)
        arrived = out_got
        if step < last:
            out_got = send_out(arrived)
        result, token = place_out(result, arrived, step, token, *then)
        return back_got, out_got, grad_states, result, token

    arrived = back_got
    back_got = head_shift(arrived, 1)
    grad_states, token = place_grad(None, arrived, 1, out_held)
    arrived = out_got
    out_got = send_out(arrived)
    result, token = place_out(None, arrived, 1, token)
    grad_states, token = place_grad(grad_states, back_held, 0, token)
    result, token = place_out(result, out_held, 0, token)
    for part in gain_parts:
        gain_part = gain_part + part
    gain_part = pass_on(gain_part, back_got)
    gain_chip = chip_columns(gain_part, 0)
    gain_far = [chip_shift(chip_columns(gain_part, k), k) for k in others]
    left, right = [near_normed], [second_left]
    grads_first = [jnp.where(encoder, grad_memory[0], grad_query)]
    grads_second = [jnp.where(encoder, grad_memory[1], context)]
    for k in others:
        pieces = jnp.split(moved[k - 1], (span, 2 * span, 2 * span + columns), axis=1)
        left.append(jnp.where(encoder, far_normed[k - 1], pieces[0]))
        right.append(jnp.where(encoder, far_normed[k - 1], pieces[1]))
        grads_first.append(jnp.where(encoder, far_memory[k - 1][0], pieces[2]))
        grads_second.append(jnp.where(encoder, far_memory[k - 1][1], pieces[3]))

    def weight_grads(half):
        def one(rows, grads):
            rows, grads = jnp.concatenate(rows, axis=0), jnp.concatenate(grads, axis=0)
            return dot_rows(lax.dynamic_slice_in_dim(rows, half * tile, tile, 1), grads)

        return one(left, grads_first), one(right, grads_second)

    halves = jnp.stack([x.astype(BF16) for x in weight_grads(1 - core)])
    swapped = core_swap(halves)
    for step in range(2, last):
        back_got, out_got, grad_states, result, token = next_round(
            step, back_got, out_got, grad_states, result, token, [gain_part], []
        )
    for part in gain_far:
        gain_chip = gain_chip + part
    gain_sum = lax.dynamic_slice_in_dim(gain_chip, core * tile, tile, 1)
    gain_sum = gain_sum + core_swap(
        lax.dynamic_slice_in_dim(gain_chip, (1 - core) * tile, tile, 1)
    )
    first_sum, second_sum = weight_grads(core)
    first_sum = first_sum + swapped[0].astype(F32)
    second_sum = second_sum + swapped[1].astype(F32)
    back_got, out_got, grad_states, result, token = next_round(
        last, back_got, out_got, grad_states, result, token, [gain_chip, halves, first_sum], [second_sum]
    )
    return (
        result[None, None],
        grad_states[None, None],
        gain_sum,
        first_sum[None],
        second_sum[None],
    )


def solution(mesh):
    return jax.shard_map(
        shards,
        mesh=mesh,
        in_specs=(
            P("section", "dp", None, None),
            P("section", None),
            P("section", "dp", "mp"),
            P("section", "dp", "mp"),
            P("dp", None),
            P("section", "dp", None, None),
        ),
        out_specs=(
            P("section", "dp", None, None),
            P("section", "dp", None, None),
            P("section", "dp"),
            P("section", "dp", "mp"),
            P("section", "dp", "mp"),
        ),
        check_vma=False,
    )
```
